256 devices in a mesh: pulse: 32 (over z, x), band: 8 (over y, core).
Axes of the slice: x: 4, y: 4, z: 8, core: 2. Of those that a mesh axis runs over, the one named last changes fastest.
Arguments:
- echoes: bfloat16 [2, 512, 32768], P(None, 'pulse', 'band'), may hold values from -6 to 6
- replica: bfloat16 [2, 2048], replicated, may hold values from -0.125 to 0.125
- pulse_angles: float32 [3, 512], replicated, may hold values from -3.140625 to 3.140625
- footprint: int32 [32, 8], replicated, may hold values from -1 to 127, as said below
- tile_slot: int32 [128], replicated, may hold values from 0 to 127, as said below
- offsets: int32 [512, 8], replicated, may hold values from 0 to 3840
Outputs:
- image_tiles: float32 [2, 128, 2048, 256], P(None, 'pulse', 'band')
- phase_gradient: float32 [512], P('pulse')
The draws below stay inside these ranges and needn't reach their ends.
Inputs may be any that keep to these rules, and one draw needn't show every extreme that they name: `footprint`: row d lists distinct tiles touched by pulse block d, live entries first and -1 after them; each row has 4 to 8 live entries and some row is full. Live entries whose tiles have the same owner (tile_slot // 4) stand next to each other in groups of 1, only the last group of a row may be shorter; some owner has 1 tiles in every row. A permutation: tile t has slot tile_slot[t], its owner is index tile_slot[t] // 4 of the pulse axis.
All inputs are finite; a program needn't handle non-finite values.
Results may differ from the reference program's by a relative error of at most 0.017.
Values may be sent and summed in bfloat16 or wider, within the bound.
No kernel may reach another device: no remote copies, remote signals or barrier semaphores. Data moves between devices by JAX's collectives and lax.ppermute only.
A program may use at most 384 MiB of HBM per device.

```python
import math
import jax
import jax.numpy as jnp
from jax import lax

TILE = 256
TAPS = 2048
RB = 4096
P_DEV = 16
FOOT = 8
TILES_DEV = 4
PULSES = 512
SAMPLES = 32768
NTILE = 128
CAP = 1
N_PULSE = 32
N_BAND = 8


def plan_tables(key):
    slots = jax.random.permutation(jax.random.fold_in(key, 11), NTILE).astype(jnp.int32)
    tile_of = jnp.zeros((NTILE,), jnp.int32).at[slots].set(jnp.arange(NTILE, dtype=jnp.int32))
    heavy_owner = jax.random.randint(jax.random.fold_in(key, 12), (), 0, N_PULSE)
    order_keys = jax.random.split(jax.random.fold_in(key, 13), N_PULSE)

    def owner_order(order_key):
        return jax.random.permutation(order_key, N_PULSE).astype(jnp.int32)
    owner_orders = jax.vmap(owner_order)(order_keys)
    leading = owner_orders[:, :1]
    owner_orders = jnp.where(owner_orders == heavy_owner, leading, owner_orders)
    owner_orders = owner_orders.at[:, 0].set(heavy_owner)
    group_count = FOOT // CAP
    owners = jnp.repeat(owner_orders[:, :group_count], CAP, axis=1)
    local_keys = jax.random.split(jax.random.fold_in(key, 14), N_PULSE * group_count)

    def local_pick(local_key):
        return jax.random.permutation(local_key, TILES_DEV)[:CAP].astype(jnp.int32)
    local_picks = jax.vmap(local_pick)(local_keys).reshape(N_PULSE, FOOT)
    tile_ids = tile_of[owners * TILES_DEV + local_picks]
    live_counts = jax.random.randint(jax.random.fold_in(key, 15), (N_PULSE,), FOOT // 2, FOOT + 1)
    full_block = jax.random.randint(jax.random.fold_in(key, 16), (), 0, N_PULSE)
    live_counts = jnp.where(jnp.arange(N_PULSE) == full_block, FOOT, live_counts)
    positions = jnp.arange(FOOT)
    listed = jnp.where(positions[None, :] < live_counts[:, None], tile_ids, -1).astype(jnp.int32)
    return (slots, listed)


def draw_footprint(key, part):
    slots, listed = plan_tables(key)
    return listed


def draw_tile_slot(key, part):
    slots, listed = plan_tables(key)
    return slots


def touch_ends(drawn, rng, low, top_value):
    extent = drawn.shape
    spot = [jax.random.randint(jax.random.fold_in(rng, axis), (), 0, extent[axis]) for axis in range(len(extent))]
    drawn = drawn.at[tuple(spot)].set(low)
    longest = extent.index(max(extent))
    spot[longest] = (spot[longest] + 1) % extent[longest]
    return drawn.at[tuple(spot)].set(top_value)


def block_levels(stream_key, extent, shards, low, high):
    def one(position, parts):
        steps = jax.random.uniform(jax.random.fold_in(jax.random.fold_in(stream_key, 6), position), (parts,), jnp.float32, low / len(shards), high / len(shards))
        return jnp.repeat(jnp.exp(steps), extent[position] // parts).reshape((-1,) + (1,) * (len(extent) - position - 1))

    gain = one(*shards[0])
    for cut in shards[1:]:
        gain = gain * one(*cut)
    return gain


def bell_draw(rng, shape, spread, most, cuts=(), held_as=jnp.bfloat16):
    values = spread * jax.random.normal(rng, shape, jnp.float32)
    if cuts:
        values = values * block_levels(rng, shape, cuts, -0.22, 0.18)
    return jnp.clip(values, -most, most).astype(held_as)


def setup_inputs(seed: int = 0) -> dict:
    seeds = jax.random.split(jax.random.key(seed), 7)
    echoes = bell_draw(seeds[0], (2, PULSES, SAMPLES), 1.0, 6.0, ((1, 32), (2, 8)))
    replica = bell_draw(seeds[1], (2, TAPS), TAPS ** -0.5, 0.125)
    pulse_angles = jnp.clip(jax.random.uniform(seeds[2], (3, PULSES), jnp.float32, -3.140625, 3.140625), -3.140625, 3.140625)
    footprint = draw_footprint(jax.random.fold_in(seeds[6], 71), 0)
    tile_slot = draw_tile_slot(jax.random.fold_in(seeds[6], 71), 0)
    offsets = touch_ends(jax.random.randint(seeds[5], (PULSES, FOOT), 0, RB - TILE + 1), jax.random.fold_in(seeds[5], 1), 0, RB - TILE).astype(jnp.int32)
    return {"echoes": echoes, "replica": replica, "pulse_angles": pulse_angles, "footprint": footprint, "tile_slot": tile_slot, "offsets": offsets}


def compress_all(echoes, replica):
    length = 1 << (SAMPLES + TAPS - 1).bit_length()
    wave = lax.complex(replica[0].astype(jnp.float32), replica[1].astype(jnp.float32))
    kernel = jnp.conj(jnp.fft.fft(wave, n=length))

    def per_group(group_data):
        signal = lax.complex(group_data[0].astype(jnp.float32), group_data[1].astype(jnp.float32))
        spectrum = jnp.fft.fft(signal, n=length, axis=-1) * kernel[None, :]
        result = jnp.fft.ifft(spectrum, axis=-1)[:, :SAMPLES]
        return jnp.stack([jnp.real(result), jnp.imag(result)]).astype(jnp.bfloat16)
    grouped = jnp.transpose(echoes.reshape(2, N_PULSE, P_DEV, SAMPLES), (1, 0, 2, 3))
    return lax.map(per_group, grouped)

def steer_table(omega):
    column = jnp.arange(TILE, dtype=jnp.float32)
    phases = omega[:, None] * column[None, :]
    cosine = jnp.cos(phases).astype(jnp.bfloat16)
    sine_part = jnp.sin(phases).astype(jnp.bfloat16)
    upper_half = jnp.stack([cosine, sine_part], axis=1)
    lower_half = jnp.stack([-sine_part, cosine], axis=1)
    return jnp.stack([upper_half, lower_half])

def pick_rows(packed, starts):

    def per_pulse(series, firsts):

        def per_slot(first_index):
            return lax.dynamic_slice_in_dim(series, first_index, TILE, 1)
        return jax.vmap(per_slot)(firsts)
    picked = jax.vmap(per_pulse, in_axes=(1, 0))(packed, starts)
    return jnp.transpose(picked, (1, 2, 0, 3))

def rotated(picked, kappa, phase, tile_ids, factor):
    rotation = kappa[None, :] * tile_ids.astype(jnp.float32)[:, None] + phase[None, :]
    cosine = jnp.cos(rotation)[:, :, None]
    sine_part = jnp.sin(rotation)[:, :, None]
    real_part = picked[:, 0].astype(jnp.float32)
    imag_part = picked[:, 1].astype(jnp.float32)
    rot_real = (real_part * cosine - imag_part * sine_part) * factor
    rot_imag = (real_part * sine_part + imag_part * cosine) * factor
    return jnp.stack([rot_real, rot_imag], axis=1).astype(jnp.bfloat16)

def sharp_weight(image_sum, comp_axis):
    real_part = jnp.take(image_sum, 0, axis=comp_axis)
    imag_part = jnp.take(image_sum, 1, axis=comp_axis)
    power = real_part * real_part + imag_part * imag_part
    return jnp.stack([power * real_part, -power * imag_part], axis=comp_axis).astype(jnp.bfloat16)

def reference(echoes, replica, pulse_angles, footprint, tile_slot, offsets):
    packed = compress_all(echoes, replica)
    banded = jnp.transpose(packed.reshape(N_PULSE, 2, P_DEV, N_BAND, RB), (0, 3, 1, 2, 4))
    angle_sets = jnp.transpose(pulse_angles.reshape(3, N_PULSE, P_DEV), (1, 0, 2))
    block_offsets = offsets.reshape(N_PULSE, P_DEV, FOOT)
    factor = 0.5 / math.sqrt(P_DEV)
    highest = lax.Precision.HIGHEST

    def first_pass(image_sum, inputs):
        series, angle_rows, starts, listed = inputs
        live_mask = listed >= 0
        safe_ids = jnp.maximum(listed, 0)

        def per_band(band_series):
            return rotated(pick_rows(band_series, starts), angle_rows[1], angle_rows[2], safe_ids, factor)
        picked_rows = jax.vmap(per_band)(series)
        steering = steer_table(angle_rows[0])
        partial_value = jnp.einsum('bkcqi,cqdj->bkdij', picked_rows.astype(jnp.float32), steering.astype(jnp.float32), precision=highest)
        partial_value = jnp.where(live_mask[None, :, None, None, None], partial_value, jnp.float32(0.0)).astype(jnp.bfloat16)
        partial_value = lax.optimization_barrier(partial_value).astype(jnp.float32)
        target = jnp.where(live_mask, safe_ids, NTILE)
        image_sum = image_sum.at[:, :, target].add(jnp.transpose(partial_value, (0, 2, 1, 3, 4)), mode='drop')
        return (image_sum, (picked_rows, steering, live_mask, safe_ids))
    start_image = jnp.zeros((N_BAND, 2, NTILE, TILE, TILE), jnp.float32)
    image_sum, stored = lax.scan(first_pass, start_image, (banded, angle_sets, block_offsets, footprint))
    weight = sharp_weight(image_sum, 1)

    def second_pass(running, stored_item):
        picked_rows, steering, live_mask, safe_ids = stored_item
        taken = jnp.take(weight, safe_ids, axis=2)
        masked = jnp.where(live_mask[None, None, :, None, None], taken, jnp.zeros_like(taken))
        projected = jnp.einsum('bckij,cqdj->bkdqi', masked.astype(jnp.float32), steering.astype(jnp.float32), precision=highest)
        rows_wide = picked_rows.astype(jnp.float32)
        terms = rows_wide[:, :, 0] * projected[:, :, 1] + rows_wide[:, :, 1] * projected[:, :, 0]
        return (running, -4.0 * lax.optimization_barrier(jnp.sum(terms, axis=(0, 1, 3))))
    _, gradients = lax.scan(second_pass, jnp.float32(0.0), stored)
    gradients = gradients.reshape(PULSES)
    phase_gradient = gradients / jnp.sqrt(jnp.sum(gradients * gradients) / PULSES + 1e-05)
    tile_of = jnp.zeros((NTILE,), jnp.int32).at[tile_slot].set(jnp.arange(NTILE, dtype=jnp.int32))
    ordered = jnp.take(image_sum, tile_of, axis=2)
    image_tiles = jnp.transpose(ordered, (1, 2, 0, 3, 4)).reshape(2, NTILE, N_BAND * TILE, TILE)
    return (image_tiles, phase_gradient)
```

```python
import math

import jax
import jax.numpy as jnp
from jax import lax
from jax.experimental import pallas as pl
from jax.experimental.pallas import tpu as pltpu
from jax.sharding import PartitionSpec as P

TILE = 256
TAPS = 2048
RB = 4096
P_DEV = 16
FOOT = 8
TILES_DEV = 4
NTILE = 128
PULSES = 512
N_PULSE = 32
N_BAND = 8
LANE = 128

SPANS = TAPS // TILE + 1
BLOCKS = RB // TILE
ROWS = BLOCKS * P_DEV
KDIM = 2 * PULSES
FACTOR = 0.5 / math.sqrt(P_DEV)

NT = (((1,), (1,)), ((), ()))
NN = (((1,), (0,)), ((), ()))

VMEM_BYTES = 48 * 1024 * 1024


def vmem():
    return pl.BlockSpec(memory_space=pltpu.VMEM)


def smem():
    return pl.BlockSpec(memory_space=pltpu.SMEM)


def taps_kernel(replica_ref, taps_ref):
    width = TAPS + LANE
    chunks = width // LANE
    sub = lax.broadcasted_iota(jnp.int32, (8, width), 0)
    zero = jnp.zeros((16, LANE), jnp.bfloat16)
    for comp in range(2):
        line = replica_ref[comp : comp + 1, :].astype(jnp.float32)
        line = jnp.concatenate([line, jnp.zeros((1, LANE), jnp.float32)], axis=1)
        wide = jnp.broadcast_to(line, (8, width))
        base = wide
        for r in range(1, 8):
            base = jnp.where(sub == r, pltpu.roll(wide, r, 1), base)
        for j in range(8):
            first = base if j == 0 else pltpu.roll(base, 16 * j, 1)
            pair = jnp.concatenate([first, pltpu.roll(base, 16 * j + 8, 1)], axis=0)
            pair = pair.astype(jnp.bfloat16)
            for half in range(2):
                row = LANE * half + 16 * j
                for c in range(2 * SPANS):
                    src = c - half
                    piece = pair[:, LANE * src : LANE * src + LANE] if 0 <= src < chunks else zero
                    col = 512 * (c // 2) + TILE * comp + LANE * (c % 2)
                    taps_ref[row : row + 16, col : col + LANE] = piece


def lane_shift(low, high, shift):
    first, second = low[:, :LANE], low[:, LANE:]
    third, fourth = high[:, :LANE], high[:, LANE:]
    far = shift >= LANE
    parts = [
        jnp.where(far, second, first),
        jnp.where(far, third, second),
        jnp.where(far, fourth, third),
    ]
    step = shift & (LANE - 1)
    lane = lax.broadcasted_iota(jnp.int32, first.shape, 1)
    index = (lane + step) & (LANE - 1)
    turned = [jnp.take_along_axis(part, index, axis=1) for part in parts]
    stay = lane < LANE - step
    return jnp.concatenate(
        [jnp.where(stay, turned[0], turned[1]), jnp.where(stay, turned[1], turned[2])], axis=1
    )


def rows_kernel(
    footprint_ref, slot_ref, echo_ref, tail_ref, taps_ref, angle_ref, offset_ref, out_ref, win_ref
):
    me = lax.axis_index("pulse")
    for n in range(BLOCKS + SPANS - 1):
        for comp in range(2):
            if n < BLOCKS:
                piece = echo_ref[comp, :, TILE * n : TILE * n + TILE]
            else:
                piece = tail_ref[comp, :, TILE * (n - BLOCKS) : TILE * (n - BLOCKS) + TILE]
            win_ref[P_DEV * n : P_DEV * n + P_DEV, TILE * comp : TILE * comp + TILE] = piece
            if comp == 0:
                win_ref[P_DEV * n : P_DEV * n + P_DEV, 2 * TILE :] = -piece
    total = jnp.zeros((2 * ROWS, TILE), jnp.float32)
    for a in range(SPANS):
        rows = slice(P_DEV * a, P_DEV * a + ROWS)
        left = jnp.concatenate([win_ref[rows, : 2 * TILE], win_ref[rows, TILE:]], axis=0)
        total += lax.dot_general(
            left, taps_ref[:, 512 * a : 512 * a + 512], NT, preferred_element_type=jnp.float32
        )
    series = jnp.concatenate([total[:ROWS], total[ROWS:]], axis=1).astype(jnp.bfloat16)

    begin = pl.multiple_of(me * P_DEV, P_DEV)
    offsets = offset_ref[pl.ds(begin, P_DEV), :]
    pulse = lax.broadcasted_iota(jnp.int32, (P_DEV, ROWS), 0)
    lane = lax.broadcasted_iota(jnp.int32, (P_DEV, ROWS), 1)
    low_hot, high_hot = [], []
    for k in range(FOOT):
        block = offsets[:, k : k + 1] >> 8
        low_hot.append(jnp.where(lane == block * P_DEV + pulse, 1.0, 0.0))
        block = jnp.minimum(block + 1, BLOCKS - 1)
        high_hot.append(jnp.where(lane == block * P_DEV + pulse, 1.0, 0.0))
    hot = jnp.concatenate(low_hot + high_hot, axis=0).astype(jnp.bfloat16)
    picked = lax.dot_general(hot, series, NN, preferred_element_type=jnp.float32)

    wide_lane = lax.broadcasted_iota(jnp.int32, (P_DEV, PULSES), 1)
    wide_sub = lax.broadcasted_iota(jnp.int32, (P_DEV, PULSES), 0)
    mine = wide_lane == begin + wide_sub
    kappa = jnp.sum(jnp.where(mine, angle_ref[1:2, :], 0.0), axis=1, keepdims=True)
    phase = jnp.sum(jnp.where(mine, angle_ref[2:3, :], 0.0), axis=1, keepdims=True)
    column = lax.broadcasted_iota(jnp.int32, (P_DEV, LANE), 1)
    tiles = [footprint_ref[me, k] for k in range(FOOT)]
    tile_row = jnp.zeros((P_DEV, LANE), jnp.float32)
    for k in range(FOOT):
        tile_row = jnp.where(column == k, jnp.maximum(tiles[k], 0).astype(jnp.float32), tile_row)
    turn = kappa * tile_row + phase
    cosine, sine = jnp.cos(turn), jnp.sin(turn)

    out_ref[...] = jnp.zeros_like(out_ref)
    for k in range(FOOT):
        low = picked[P_DEV * k : P_DEV * k + P_DEV]
        high = picked[P_DEV * (FOOT + k) : P_DEV * (FOOT + k) + P_DEV]
        shift = jnp.broadcast_to(offsets[:, k : k + 1] & (TILE - 1), (P_DEV, LANE))
        real = lane_shift(low[:, :TILE], high[:, :TILE], shift)
        imag = lane_shift(low[:, TILE:], high[:, TILE:], shift)
        c, s = cosine[:, k : k + 1], sine[:, k : k + 1]
        rot_real = ((real * c - imag * s) * FACTOR).astype(jnp.bfloat16)
        rot_imag = ((real * s + imag * c) * FACTOR).astype(jnp.bfloat16)
        owner = slot_ref[jnp.maximum(tiles[k], 0)] >> 2

        @pl.when(tiles[k] >= 0)
        def _():
            out_ref[owner, 0] = rot_real
            out_ref[owner, 1] = rot_imag


def steer_kernel(footprint_ref, slot_ref, angle_ref, steer_ref, local_ref):
    me = lax.axis_index("pulse")

    def per_block(d, carry):
        found = jnp.int32(-1)
        for k in range(FOOT):
            tile = footprint_ref[d, k]
            slot = slot_ref[jnp.maximum(tile, 0)]
            found = jnp.where((tile >= 0) & ((slot >> 2) == me), slot & 3, found)
        local_ref[d] = found
        return carry

    lax.fori_loop(0, N_PULSE, per_block, 0)

    def per_rows(g, carry):
        begin = pl.multiple_of(g * 16, 16)
        j = (begin + lax.broadcasted_iota(jnp.int32, (16, PULSES), 0)).astype(jnp.float32)
        phases = j * angle_ref[0:1, :]
        cosine = jnp.cos(phases).astype(jnp.bfloat16)
        sine = jnp.sin(phases).astype(jnp.bfloat16)
        steer_ref[pl.ds(begin, 16), :PULSES] = cosine
        steer_ref[pl.ds(begin, 16), PULSES:] = -sine
        lower = pl.multiple_of(TILE + g * 16, 16)
        steer_ref[pl.ds(lower, 16), :PULSES] = sine
        steer_ref[pl.ds(lower, 16), PULSES:] = cosine
        return carry

    lax.fori_loop(0, TILE // 16, per_rows, 0)


def owner_kernel(local_ref, arrived_ref, steer_ref, image_ref, grad_ref, rows_ref, weight_ref):
    for d in range(N_PULSE):
        slot = local_ref[d]
        for comp in range(2):
            piece = arrived_ref[d, comp]
            row = PULSES * comp + P_DEV * d
            for l in range(TILES_DEV):
                rows_ref[row : row + P_DEV, TILE * l : TILE * l + TILE] = jnp.where(
                    slot == l, piece, jnp.zeros_like(piece)
                )
    for l in range(TILES_DEV):
        cols = slice(TILE * l, TILE * l + TILE)
        total = lax.dot_general(
            steer_ref[...], rows_ref[:, cols], NN, preferred_element_type=jnp.float32
        )
        image_ref[:, cols] = total
        real, imag = total[:TILE], total[TILE:]
        power = real * real + imag * imag
        weight_ref[:TILE, cols] = (-power * imag).astype(jnp.bfloat16)
        weight_ref[TILE:, cols] = (power * real).astype(jnp.bfloat16)
    sums = []
    for h in range(KDIM // TILE):
        cols = slice(TILE * h, TILE * h + TILE)
        back = lax.dot_general(
            weight_ref[...], rows_ref[cols, :], NT, preferred_element_type=jnp.float32
        )
        sums.append(
            jnp.sum(back * steer_ref[:, cols].astype(jnp.float32), axis=0, keepdims=True)
        )
    halves = [-4.0 * (sums[h] + sums[h + 2]) for h in range(2)]
    for c in range(PULSES // LANE):
        piece = halves[c // 2][:, LANE * (c % 2) : LANE * (c % 2) + LANE]
        for b in range(N_BAND):
            grad_ref[b, c : c + 1, :] = piece


def image_kernel(flat_ref, out_ref):
    out_ref[0, 0] = flat_ref[...].T


def params():
    return pltpu.CompilerParams(vmem_limit_bytes=VMEM_BYTES)


def on_device(echoes, replica, pulse_angles, footprint, tile_slot, offsets):
    me = lax.axis_index("pulse")
    pairs = [(i, i - 1) for i in range(1, N_BAND)]
    tail = lax.ppermute(echoes, "band", pairs)
    taps = pl.pallas_call(
        taps_kernel,
        out_shape=jax.ShapeDtypeStruct((TILE, 2 * TILE * SPANS), jnp.bfloat16),
        in_specs=[vmem()],
        out_specs=vmem(),
        compiler_params=params(),
        cost_estimate=pl.CostEstimate(flops=0, bytes_accessed=8 << 20, transcendentals=0),
        name="taps",
    )(replica)
    rows = pl.pallas_call(
        rows_kernel,
        grid=(1,),
        out_shape=jax.ShapeDtypeStruct((N_PULSE, 2, P_DEV, TILE), jnp.bfloat16),
        in_specs=[
            smem(),
            smem(),
            vmem(),
            pl.BlockSpec((2, P_DEV, TAPS), lambda g: (0, 0, 0)),
            vmem(),
            vmem(),
            vmem(),
        ],
        out_specs=vmem(),
        scratch_shapes=[pltpu.VMEM((ROWS + P_DEV * (SPANS - 1), 3 * TILE), jnp.bfloat16)],
        compiler_params=params(),
        name="rows",
    )(footprint, tile_slot, echoes, tail, taps, pulse_angles, offsets)
    steer, local = pl.pallas_call(
        steer_kernel,
        out_shape=[
            jax.ShapeDtypeStruct((2 * TILE, KDIM), jnp.bfloat16),
            jax.ShapeDtypeStruct((N_PULSE,), jnp.int32),
        ],
        in_specs=[smem(), smem(), vmem()],
        out_specs=[vmem(), smem()],
        compiler_params=params(),
        cost_estimate=pl.CostEstimate(flops=0, bytes_accessed=20 << 20, transcendentals=0),
        name="steer",
    )(footprint, tile_slot, pulse_angles)
    arrived = lax.all_to_all(rows, "pulse", split_axis=0, concat_axis=0, tiled=True)
    image_flat, grad = pl.pallas_call(
        owner_kernel,
        out_shape=[
            jax.ShapeDtypeStruct((2 * TILE, TILES_DEV * TILE), jnp.float32),
            jax.ShapeDtypeStruct((N_BAND, PULSES // LANE, LANE), jnp.float32),
        ],
        in_specs=[smem(), vmem(), vmem()],
        out_specs=[vmem(), vmem()],
        scratch_shapes=[
            pltpu.VMEM((KDIM, TILES_DEV * TILE), jnp.bfloat16),
            pltpu.VMEM((2 * TILE, TILES_DEV * TILE), jnp.bfloat16),
        ],
        compiler_params=params(),
        name="owner",
    )(local, arrived, steer)
    image = pl.pallas_call(
        image_kernel,
        grid=(2, TILES_DEV),
        out_shape=jax.ShapeDtypeStruct((2, TILES_DEV, TILE, TILE), jnp.float32),
        in_specs=[pl.BlockSpec((TILE, TILE), lambda c, l: (c, l))],
        out_specs=pl.BlockSpec((1, 1, TILE, TILE), lambda c, l: (c, l, 0, 0)),
        compiler_params=params(),
        name="image",
    )(image_flat)
    band_all = lax.all_to_all(grad, "band", split_axis=0, concat_axis=0, tiled=True)
    band_sum = jnp.sum(band_all, axis=0, keepdims=True)
    spread = jnp.broadcast_to(band_sum, (N_PULSE, PULSES // LANE, LANE))
    pulse_all = lax.all_to_all(spread, "pulse", split_axis=0, concat_axis=0, tiled=True)
    gradient = jnp.sum(pulse_all, axis=0)
    scaled = gradient / jnp.sqrt(jnp.sum(gradient * gradient) / PULSES + 1e-05)
    phase_gradient = lax.dynamic_slice_in_dim(scaled.reshape(PULSES), me * P_DEV, P_DEV, 0)
    return (image, phase_gradient)


def solution(mesh):
    placed = (P(None, "pulse", "band"), P(), P(), P(), P(), P())
    return jax.shard_map(
        on_device,
        mesh=mesh,
        in_specs=placed,
        out_specs=(P(None, "pulse", "band", None), P("pulse")),
        check_vma=False,
    )
```

```python
import math

import jax
import jax.numpy as jnp
from jax import lax
from jax.experimental import pallas as pl
from jax.experimental.pallas import tpu as pltpu
from jax.sharding import PartitionSpec as P

TILE = 256
TAPS = 2048
RB = 4096
P_DEV = 16
FOOT = 8
TILES_DEV = 4
NTILE = 128
PULSES = 512
N_PULSE = 32
N_BAND = 8
LANE = 128

SPANS = TAPS // TILE + 1
BLOCKS = RB // TILE
ROWS = BLOCKS * P_DEV
KDIM = 2 * PULSES
FACTOR = 0.5 / math.sqrt(P_DEV)

NT = (((1,), (1,)), ((), ()))
NN = (((1,), (0,)), ((), ()))

VMEM_BYTES = 24 * 1024 * 1024


def taps_kernel(replica_ref, taps_ref):
    width = TAPS + LANE
    chunks = width // LANE
    sub = lax.broadcasted_iota(jnp.int32, (8, width), 0)
    zero = jnp.zeros((16, LANE), jnp.bfloat16)
    for comp in range(2):
        line = replica_ref[comp : comp + 1, :].astype(jnp.float32)
        line = jnp.concatenate([line, jnp.zeros((1, LANE), jnp.float32)], axis=1)
        wide = jnp.broadcast_to(line, (8, width))
        base = wide
        for r in range(1, 8):
            base = jnp.where(sub == r, pltpu.roll(wide, r, 1), base)
        for j in range(8):
            first = base if j == 0 else pltpu.roll(base, 16 * j, 1)
            pair = jnp.concatenate([first, pltpu.roll(base, 16 * j + 8, 1)], axis=0)
            pair = pair.astype(jnp.bfloat16)
            for half in range(2):
                row = LANE * half + 16 * j
                for c in range(2 * SPANS):
                    src = c - half
                    piece = pair[:, LANE * src : LANE * src + LANE] if 0 <= src < chunks else zero
                    col = 512 * (c // 2) + TILE * comp + LANE * (c % 2)
                    taps_ref[row : row + 16, col : col + LANE] = piece


def fill_steer(angle_ref, steer_ref):
    step = lax.broadcasted_iota(jnp.int32, (16, PULSES), 0).astype(jnp.float32)
    omega = angle_ref[0:1, :]
    fine, coarse = step * omega, (16.0 * step) * omega
    fine_cos, fine_sin = jnp.cos(fine), jnp.sin(fine)
    coarse_cos, coarse_sin = jnp.cos(coarse), jnp.sin(coarse)
    for a in range(TILE // 16):
        ca, sa = coarse_cos[a : a + 1], coarse_sin[a : a + 1]
        cosine = (fine_cos * ca - fine_sin * sa).astype(jnp.bfloat16)
        sine = (fine_sin * ca + fine_cos * sa).astype(jnp.bfloat16)
        upper, lower = slice(16 * a, 16 * a + 16), slice(TILE + 16 * a, TILE + 16 * a + 16)
        steer_ref[upper, :PULSES] = cosine
        steer_ref[upper, PULSES:] = -sine
        steer_ref[lower, :PULSES] = sine
        steer_ref[lower, PULSES:] = cosine


def own_lanes():
    lane = lax.broadcasted_iota(jnp.int32, (P_DEV, PULSES), 1)
    sub = lax.broadcasted_iota(jnp.int32, (P_DEV, PULSES), 0)
    return lane == lax.axis_index("pulse") * P_DEV + sub


def prep_kernel(
    taps_ref,
    echo_ref,
    angle_ref,
    footprint_ref,
    slot_ref,
    offset_ref,
    steer_ref,
    slots_ref,
    local_ref,
    hot_ref,
    shift_ref,
    turn_ref,
    near_ref,
    win_ref,
    listed_ref,
):
    me = lax.axis_index("pulse")
    fill_steer(angle_ref, steer_ref)

    for n in range(BLOCKS):
        rows = slice(P_DEV * n, P_DEV * n + P_DEV)
        real = echo_ref[0, :, TILE * n : TILE * n + TILE]
        win_ref[rows, :TILE] = real
        win_ref[rows, TILE : 2 * TILE] = echo_ref[1, :, TILE * n : TILE * n + TILE]
        win_ref[rows, 2 * TILE :] = -real
    win_ref[ROWS:, :] = jnp.zeros((P_DEV * (SPANS - 1), 3 * TILE), jnp.bfloat16)
    correlate(win_ref, taps_ref, near_ref, 0, 0, None)

    listed = jnp.concatenate([footprint_ref[...], jnp.full((FOOT, LANE - N_PULSE), -1)], axis=1)
    listed = listed.T
    listed_ref[...] = listed
    lane = lax.broadcasted_iota(jnp.int32, (N_PULSE, LANE), 1)
    slots = jnp.zeros((N_PULSE, LANE), jnp.int32)
    local = jnp.zeros((N_PULSE, 1), jnp.int32)
    for k in range(FOOT):
        same = listed[:N_PULSE, k : k + 1] == lane
        slot = jnp.sum(jnp.where(same, slot_ref[...] + 1, 0), axis=1, keepdims=True)
        slots = jnp.where(lane == k, slot, slots)
        owned = (slot > 0) & (((slot - 1) >> 2) == me)
        local = jnp.where(owned, ((slot - 1) & 3) + 1, local)
    slots_ref[...] = slots
    local_ref[...] = jnp.broadcast_to(local, (N_PULSE, LANE))

    mine = own_lanes()
    tiles = jnp.maximum(listed_ref[pl.ds(me, 1), :], 0).astype(jnp.float32)
    kappa = jnp.sum(jnp.where(mine, angle_ref[1:2, :], 0.0), axis=1, keepdims=True)
    phase = jnp.sum(jnp.where(mine, angle_ref[2:3, :], 0.0), axis=1, keepdims=True)
    turn = kappa * tiles + phase
    cosine, sine = jnp.cos(turn), jnp.sin(turn)
    pulse = lax.broadcasted_iota(jnp.int32, (P_DEV, ROWS), 0)
    pick = lax.broadcasted_iota(jnp.int32, (P_DEV, ROWS), 1)
    low_hot, high_hot = [], []
    for k in range(FOOT):
        rows = slice(P_DEV * k, P_DEV * k + P_DEV)
        offset = jnp.sum(jnp.where(mine, offset_ref[k : k + 1, :], 0), axis=1, keepdims=True)
        block = offset >> 8
        low_hot.append(jnp.where(pick == block * P_DEV + pulse, 1.0, 0.0))
        block = jnp.minimum(block + 1, BLOCKS - 1)
        high_hot.append(jnp.where(pick == block * P_DEV + pulse, 1.0, 0.0))
        shift_ref[rows, :] = jnp.broadcast_to(offset & (TILE - 1), (P_DEV, LANE))
        turn_ref[0, rows, :] = jnp.broadcast_to(cosine[:, k : k + 1], (P_DEV, LANE))
        turn_ref[1, rows, :] = jnp.broadcast_to(sine[:, k : k + 1], (P_DEV, LANE))
    hot_ref[...] = jnp.concatenate(low_hot + high_hot, axis=0).astype(jnp.bfloat16)


def correlate(win_ref, taps_ref, out_ref, first_row, first_span, add_ref):
    count = out_ref.shape[1]
    spans = range(first_span, SPANS)
    taps = taps_ref[:, 512 * first_span :]
    for comp in range(2):
        cols = slice(TILE * comp, TILE * comp + 2 * TILE)
        left = [
            win_ref[first_row + P_DEV * a : first_row + P_DEV * a + count, cols] for a in spans
        ]
        total = lax.dot_general(
            jnp.concatenate(left, axis=1), taps, NT, preferred_element_type=jnp.float32
        )
        out_ref[comp] = total if add_ref is None else total + add_ref[comp, first_row:, :]


def lane_shift(low, high, shift):
    first, second = low[:, :LANE], low[:, LANE:]
    third, fourth = high[:, :LANE], high[:, LANE:]
    far = shift >= LANE
    parts = [
        jnp.where(far, second, first),
        jnp.where(far, third, second),
        jnp.where(far, fourth, third),
    ]
    step = shift & (LANE - 1)
    lane = lax.broadcasted_iota(jnp.int32, first.shape, 1)
    index = (lane + step) & (LANE - 1)
    turned = [jnp.take_along_axis(part, index, axis=1) for part in parts]
    stay = lane < LANE - step
    return jnp.concatenate(
        [jnp.where(stay, turned[0], turned[1]), jnp.where(stay, turned[1], turned[2])], axis=1
    )


def rows_kernel(
    tail_ref,
    taps_ref,
    near_ref,
    hot_ref,
    shift_ref,
    turn_ref,
    slots_ref,
    out_ref,
    win_ref,
    far_ref,
):
    me = lax.axis_index("pulse")
    half = (BLOCKS - SPANS + 1) * P_DEV
    win_ref[:ROWS, :] = jnp.zeros((ROWS, 3 * TILE), jnp.bfloat16)
    for n in range(SPANS - 1):
        rows = slice(ROWS + P_DEV * n, ROWS + P_DEV * n + P_DEV)
        real = tail_ref[0, :, TILE * n : TILE * n + TILE]
        win_ref[rows, :TILE] = real
        win_ref[rows, TILE : 2 * TILE] = tail_ref[1, :, TILE * n : TILE * n + TILE]
        win_ref[rows, 2 * TILE :] = -real
    correlate(win_ref, taps_ref, far_ref, half, 1, near_ref)
    series = jnp.concatenate(
        [
            jnp.concatenate([near_ref[0, :half, :], near_ref[1, :half, :]], axis=1),
            jnp.concatenate([far_ref[0], far_ref[1]], axis=1),
        ],
        axis=0,
    ).astype(jnp.bfloat16)
    picked = lax.dot_general(hot_ref[...], series, NN, preferred_element_type=jnp.float32)
    out_ref[...] = jnp.zeros_like(out_ref)
    for k in range(FOOT):
        rows = slice(P_DEV * k, P_DEV * k + P_DEV)
        low = picked[P_DEV * k : P_DEV * k + P_DEV]
        high = picked[P_DEV * (FOOT + k) : P_DEV * (FOOT + k) + P_DEV]
        shift = shift_ref[rows, :]
        real = lane_shift(low[:, :TILE], high[:, :TILE], shift)
        imag = lane_shift(low[:, TILE:], high[:, TILE:], shift)
        c = jnp.concatenate([turn_ref[0, rows, :]] * 2, axis=1)
        s = jnp.concatenate([turn_ref[1, rows, :]] * 2, axis=1)
        rot_real = ((real * c - imag * s) * FACTOR).astype(jnp.bfloat16)
        rot_imag = ((real * s + imag * c) * FACTOR).astype(jnp.bfloat16)
        slot = slots_ref[me, k]

        @pl.when(slot > 0)
        def _():
            owner = (slot - 1) >> 2
            out_ref[owner, 0] = rot_real
            out_ref[owner, 1] = rot_imag


def owner_kernel(local_ref, arrived_ref, steer_ref, image_ref, grad_ref, rows_ref, weight_ref):
    for d in range(N_PULSE):
        slot = local_ref[d, 0]
        for comp in range(2):
            piece = arrived_ref[d, comp]
            row = PULSES * comp + P_DEV * d
            for l in range(TILES_DEV):
                rows_ref[row : row + P_DEV, TILE * l : TILE * l + TILE] = jnp.where(
                    slot == l + 1, piece, jnp.zeros_like(piece)
                )
    for l in range(TILES_DEV):
        cols = slice(TILE * l, TILE * l + TILE)
        total = lax.dot_general(
            steer_ref[...], rows_ref[:, cols], NN, preferred_element_type=jnp.float32
        )
        image_ref[:, cols] = total
        real, imag = total[:TILE], total[TILE:]
        power = real * real + imag * imag
        weight_ref[:TILE, cols] = (-power * imag).astype(jnp.bfloat16)
        weight_ref[TILE:, cols] = (power * real).astype(jnp.bfloat16)
    sums = []
    for h in range(KDIM // TILE):
        cols = slice(TILE * h, TILE * h + TILE)
        back = lax.dot_general(
            weight_ref[...], rows_ref[cols, :], NT, preferred_element_type=jnp.float32
        )
        sums.append(
            jnp.sum(back * steer_ref[:, cols].astype(jnp.float32), axis=0, keepdims=True)
        )
    halves = [-4.0 * (sums[h] + sums[h + 2]) for h in range(2)]
    for c in range(PULSES // LANE):
        piece = halves[c // 2][:, LANE * (c % 2) : LANE * (c % 2) + LANE]
        for b in range(N_BAND):
            grad_ref[b, c : c + 1, :] = piece


def image_kernel(flat_ref, out_ref):
    for comp in range(2):
        out_ref[comp, 0] = flat_ref[TILE * comp : TILE * comp + TILE, :].T


def spread_kernel(bands_ref, out_ref):
    total = jnp.sum(bands_ref[...], axis=0)
    for m in range(N_PULSE):
        out_ref[m] = total


def final_kernel(parts_ref, out_ref):
    me = lax.axis_index("pulse")
    gradient = jnp.sum(parts_ref[...], axis=0)
    square = jnp.sum(jnp.sum(gradient * gradient, axis=0, keepdims=True), axis=1, keepdims=True)
    scaled = gradient / jnp.sqrt(square / PULSES + 1e-05)
    row = lax.broadcasted_iota(jnp.int32, scaled.shape, 0)
    own = jnp.sum(jnp.where(row == me >> 3, scaled, 0.0), axis=0, keepdims=True)
    turned = pltpu.roll(jnp.broadcast_to(own, (8, LANE)), (LANE - P_DEV * (me & 7)) & (LANE - 1), 1)
    out_ref[...] = turned[:1, :P_DEV]


def kernel(body, name, out_shape, scratch=(), cost=None, **extra):
    return pl.pallas_call(
        body,
        out_shape=out_shape,
        scratch_shapes=list(scratch),
        compiler_params=pltpu.CompilerParams(vmem_limit_bytes=VMEM_BYTES),
        cost_estimate=pl.CostEstimate(flops=0, bytes_accessed=cost, transcendentals=0) if cost else None,
        name=name,
        **extra,
    )


def on_device(echoes, replica, pulse_angles, footprint, tile_slot, offsets):
    bf16, f32, i32 = jnp.bfloat16, jnp.float32, jnp.int32
    shape = jax.ShapeDtypeStruct
    window = pltpu.VMEM((ROWS + P_DEV * (SPANS - 1), 3 * TILE), bf16)
    tail = lax.ppermute(echoes, "band", [(i, i - 1) for i in range(1, N_BAND)])
    taps = kernel(
        taps_kernel, "taps", shape((TILE, 2 * TILE * SPANS), bf16), cost=8 << 20
    )(replica)
    steer, slots, local, hot, shift, turn, near = kernel(
        prep_kernel,
        "prep",
        [
            shape((2 * TILE, KDIM), bf16),
            shape((N_PULSE, LANE), i32),
            shape((N_PULSE, LANE), i32),
            shape((ROWS, ROWS), bf16),
            shape((ROWS // 2, LANE), i32),
            shape((2, ROWS // 2, LANE), f32),
            shape((2, ROWS, TILE), f32),
        ],
        scratch=[window, pltpu.VMEM((LANE, FOOT), i32)],
        cost=12 << 20,
    )(taps, echoes, pulse_angles, footprint.T, tile_slot.reshape(1, NTILE), offsets.T)
    rows = kernel(
        rows_kernel,
        "rows",
        shape((N_PULSE, 2, P_DEV, TILE), bf16),
        scratch=[window, pltpu.VMEM((2, (SPANS - 1) * P_DEV, TILE), f32)],
    )(tail, taps, near, hot, shift, turn, slots)
    arrived = lax.all_to_all(rows, "pulse", split_axis=0, concat_axis=0, tiled=True)
    image_flat, grad = kernel(
        owner_kernel,
        "owner",
        [
            shape((2 * TILE, TILES_DEV * TILE), f32),
            shape((N_BAND, PULSES // LANE, LANE), f32),
        ],
        scratch=[
            pltpu.VMEM((KDIM, TILES_DEV * TILE), bf16),
            pltpu.VMEM((2 * TILE, TILES_DEV * TILE), bf16),
        ],
    )(local, arrived, steer)
    image = kernel(
        image_kernel,
        "image",
        shape((2, TILES_DEV, TILE, TILE), f32),
        grid=(TILES_DEV,),
        in_specs=[pl.BlockSpec((2 * TILE, TILE), lambda l: (0, l))],
        out_specs=pl.BlockSpec((2, 1, TILE, TILE), lambda l: (0, l, 0, 0)),
    )(image_flat)
    bands = lax.all_to_all(grad, "band", split_axis=0, concat_axis=0, tiled=True)
    spread = kernel(spread_kernel, "spread", shape((N_PULSE, PULSES // LANE, LANE), f32))(bands)
    parts = lax.all_to_all(spread, "pulse", split_axis=0, concat_axis=0, tiled=True)
    own = kernel(final_kernel, "final", shape((1, P_DEV), f32))(parts)
    return (image, own.reshape(P_DEV))


def solution(mesh):
    placed = (P(None, "pulse", "band"), P(), P(), P(), P(), P())
    return jax.shard_map(
        on_device,
        mesh=mesh,
        in_specs=placed,
        out_specs=(P(None, "pulse", "band", None), P("pulse")),
        check_vma=False,
    )
```

```python
import math

import jax
import jax.numpy as jnp
from jax import lax
from jax.experimental import pallas as pl
from jax.experimental.pallas import tpu as pltpu
from jax.sharding import PartitionSpec as P

TILE = 256
TAPS = 2048
RB = 4096
P_DEV = 16
FOOT = 8
TILES_DEV = 4
NTILE = 128
PULSES = 512
N_PULSE = 32
N_BAND = 8
LANE = 128

SPANS = TAPS // TILE + 1
BLOCKS = RB // TILE
ROWS = BLOCKS * P_DEV
KDIM = 2 * PULSES
FACTOR = 0.5 / math.sqrt(P_DEV)

NT = (((1,), (1,)), ((), ()))
NN = (((1,), (0,)), ((), ()))

VMEM_BYTES = 24 * 1024 * 1024


def taps_kernel(replica_ref, taps_ref):
    width = TAPS + LANE
    chunks = width // LANE
    zero = jnp.zeros((16, LANE), jnp.bfloat16)
    for comp in range(2):
        line = replica_ref[comp : comp + 1, :].astype(jnp.float32)
        line = jnp.concatenate([line, jnp.zeros((1, LANE), jnp.float32)], axis=1)
        wide = jnp.broadcast_to(line, (8, width))
        base = pltpu.roll(wide, 0, 1, stride=1, stride_axis=0)
        for j in range(8):
            first = base if j == 0 else pltpu.roll(base, 16 * j, 1)
            pair = jnp.concatenate([first, pltpu.roll(base, 16 * j + 8, 1)], axis=0)
            pair = pair.astype(jnp.bfloat16)
            for half in range(2):
                row = LANE * half + 16 * j
                for c in range(2 * SPANS):
                    src = c - half
                    piece = pair[:, LANE * src : LANE * src + LANE] if 0 <= src < chunks else zero
                    col = 512 * (c // 2) + TILE * comp + LANE * (c % 2)
                    taps_ref[row : row + 16, col : col + LANE] = piece


def fill_steer(angle_ref, steer_ref):
    step = lax.broadcasted_iota(jnp.int32, (16, PULSES), 0).astype(jnp.float32)
    omega = angle_ref[0:1, :]
    fine, coarse = step * omega, (16.0 * step) * omega
    fine_cos, fine_sin = jnp.cos(fine), jnp.sin(fine)
    coarse_cos, coarse_sin = jnp.cos(coarse), jnp.sin(coarse)
    for a in range(TILE // 16):
        ca, sa = coarse_cos[a : a + 1], coarse_sin[a : a + 1]
        cosine = (fine_cos * ca - fine_sin * sa).astype(jnp.bfloat16)
        sine = (fine_sin * ca + fine_cos * sa).astype(jnp.bfloat16)
        upper, lower = slice(16 * a, 16 * a + 16), slice(TILE + 16 * a, TILE + 16 * a + 16)
        steer_ref[upper, :PULSES] = cosine
        steer_ref[upper, PULSES:] = -sine
        steer_ref[lower, :PULSES] = sine
        steer_ref[lower, PULSES:] = cosine


def own_lanes():
    lane = lax.broadcasted_iota(jnp.int32, (P_DEV, PULSES), 1)
    sub = lax.broadcasted_iota(jnp.int32, (P_DEV, PULSES), 0)
    return lane == lax.axis_index("pulse") * P_DEV + sub


def prep_kernel(
    taps_ref,
    echo_ref,
    angle_ref,
    footprint_ref,
    slot_ref,
    offset_ref,
    steer_ref,
    slots_ref,
    local_ref,
    hot_ref,
    shift_ref,
    turn_ref,
    near_ref,
    win_ref,
    listed_ref,
):
    me = lax.axis_index("pulse")
    fill_steer(angle_ref, steer_ref)

    for n in range(BLOCKS):
        rows = slice(P_DEV * n, P_DEV * n + P_DEV)
        real = echo_ref[0, :, TILE * n : TILE * n + TILE]
        win_ref[rows, :TILE] = real
        win_ref[rows, TILE : 2 * TILE] = echo_ref[1, :, TILE * n : TILE * n + TILE]
        win_ref[rows, 2 * TILE :] = -real
    win_ref[ROWS:, :] = jnp.zeros((P_DEV * (SPANS - 1), 3 * TILE), jnp.bfloat16)
    correlate(win_ref, taps_ref, near_ref, 0, 0, None)

    listed = jnp.concatenate([footprint_ref[...], jnp.full((FOOT, LANE - N_PULSE), -1)], axis=1)
    listed = listed.T
    listed_ref[...] = listed
    lane = lax.broadcasted_iota(jnp.int32, (N_PULSE, LANE), 1)
    slots = jnp.zeros((N_PULSE, LANE), jnp.int32)
    local = jnp.zeros((N_PULSE, 1), jnp.int32)
    for k in range(FOOT):
        same = listed[:N_PULSE, k : k + 1] == lane
        slot = jnp.sum(jnp.where(same, slot_ref[...] + 1, 0), axis=1, keepdims=True)
        slots = jnp.where(lane == k, slot, slots)
        owned = (slot > 0) & (((slot - 1) >> 2) == me)
        local = jnp.where(owned, ((slot - 1) & 3) + 1, local)
    slots_ref[...] = slots
    local_ref[...] = jnp.broadcast_to(local, (N_PULSE, LANE))

    mine = own_lanes()
    tiles = jnp.maximum(listed_ref[pl.ds(me, 1), :], 0).astype(jnp.float32)
    kappa = jnp.sum(jnp.where(mine, angle_ref[1:2, :], 0.0), axis=1, keepdims=True)
    phase = jnp.sum(jnp.where(mine, angle_ref[2:3, :], 0.0), axis=1, keepdims=True)
    turn = kappa * tiles + phase
    cosine, sine = jnp.cos(turn), jnp.sin(turn)
    pulse = lax.broadcasted_iota(jnp.int32, (P_DEV, ROWS), 0)
    pick = lax.broadcasted_iota(jnp.int32, (P_DEV, ROWS), 1)
    low_hot, high_hot = [], []
    for k in range(FOOT):
        rows = slice(P_DEV * k, P_DEV * k + P_DEV)
        offset = jnp.sum(jnp.where(mine, offset_ref[k : k + 1, :], 0), axis=1, keepdims=True)
        block = offset >> 8
        low_hot.append(jnp.where(pick == block * P_DEV + pulse, 1.0, 0.0))
        block = jnp.minimum(block + 1, BLOCKS - 1)
        high_hot.append(jnp.where(pick == block * P_DEV + pulse, 1.0, 0.0))
        shift_ref[rows, :] = jnp.broadcast_to(offset & (TILE - 1), (P_DEV, LANE))
        turn_ref[0, rows, :] = jnp.broadcast_to(cosine[:, k : k + 1], (P_DEV, LANE))
        turn_ref[1, rows, :] = jnp.broadcast_to(sine[:, k : k + 1], (P_DEV, LANE))
    hot_ref[...] = jnp.concatenate(low_hot + high_hot, axis=0).astype(jnp.bfloat16)


def correlate(win_ref, taps_ref, out_ref, first_row, first_span, add_ref):
    count = out_ref.shape[1]
    left = []
    for comp in range(2):
        cols = slice(TILE * comp, TILE * comp + 2 * TILE)
        spans = [
            win_ref[first_row + P_DEV * a : first_row + P_DEV * a + count, cols]
            for a in range(first_span, SPANS)
        ]
        left.append(jnp.concatenate(spans, axis=1))
    total = lax.dot_general(
        jnp.concatenate(left, axis=0),
        taps_ref[:, 2 * TILE * first_span :],
        NT,
        preferred_element_type=jnp.float32,
    )
    for comp in range(2):
        part = total[count * comp : count * comp + count]
        out_ref[comp] = part if add_ref is None else part + add_ref[comp, first_row:, :]


def lane_shift(low, high, shift):
    first, second = low[:, :LANE], low[:, LANE:]
    third, fourth = high[:, :LANE], high[:, LANE:]
    far = shift >= LANE
    parts = [
        jnp.where(far, second, first),
        jnp.where(far, third, second),
        jnp.where(far, fourth, third),
    ]
    step = shift & (LANE - 1)
    lane = lax.broadcasted_iota(jnp.int32, first.shape, 1)
    index = (lane + step) & (LANE - 1)
    turned = [jnp.take_along_axis(part, index, axis=1) for part in parts]
    stay = lane < LANE - step
    return jnp.concatenate(
        [jnp.where(stay, turned[0], turned[1]), jnp.where(stay, turned[1], turned[2])], axis=1
    )


def rows_kernel(
    tail_ref,
    taps_ref,
    near_ref,
    hot_ref,
    shift_ref,
    turn_ref,
    slots_ref,
    out_ref,
    win_ref,
    far_ref,
):
    me = lax.axis_index("pulse")
    half = (BLOCKS - SPANS + 1) * P_DEV
    win_ref[:ROWS, :] = jnp.zeros((ROWS, 3 * TILE), jnp.bfloat16)
    for n in range(SPANS - 1):
        rows = slice(ROWS + P_DEV * n, ROWS + P_DEV * n + P_DEV)
        real = tail_ref[0, :, TILE * n : TILE * n + TILE]
        win_ref[rows, :TILE] = real
        win_ref[rows, TILE : 2 * TILE] = tail_ref[1, :, TILE * n : TILE * n + TILE]
        win_ref[rows, 2 * TILE :] = -real
    correlate(win_ref, taps_ref, far_ref, half, 1, near_ref)
    series = jnp.concatenate(
        [
            jnp.concatenate([near_ref[0, :half, :], near_ref[1, :half, :]], axis=1),
            jnp.concatenate([far_ref[0], far_ref[1]], axis=1),
        ],
        axis=0,
    ).astype(jnp.bfloat16)
    picked = lax.dot_general(hot_ref[...], series, NN, preferred_element_type=jnp.float32)
    out_ref[...] = jnp.zeros_like(out_ref)
    for k in reversed(range(FOOT)):
        rows = slice(P_DEV * k, P_DEV * k + P_DEV)
        low = picked[P_DEV * k : P_DEV * k + P_DEV]
        high = picked[P_DEV * (FOOT + k) : P_DEV * (FOOT + k) + P_DEV]
        shift = shift_ref[rows, :]
        real = lane_shift(low[:, :TILE], high[:, :TILE], shift)
        imag = lane_shift(low[:, TILE:], high[:, TILE:], shift)
        c = jnp.concatenate([turn_ref[0, rows, :]] * 2, axis=1)
        s = jnp.concatenate([turn_ref[1, rows, :]] * 2, axis=1)
        slot = slots_ref[me, k]
        owner = (jnp.where(slot > 0, slot, slots_ref[me, 0]) - 1) >> 2
        out_ref[owner, 0] = ((real * c - imag * s) * FACTOR).astype(jnp.bfloat16)
        out_ref[owner, 1] = ((real * s + imag * c) * FACTOR).astype(jnp.bfloat16)


def owner_kernel(local_ref, arrived_ref, steer_ref, image_ref, grad_ref, rows_ref, weight_ref):
    for d in range(N_PULSE):
        slot = local_ref[d, 0]
        for comp in range(2):
            piece = arrived_ref[d, comp]
            row = PULSES * comp + P_DEV * d
            for l in range(TILES_DEV):
                rows_ref[row : row + P_DEV, TILE * l : TILE * l + TILE] = jnp.where(
                    slot == l + 1, piece, jnp.zeros_like(piece)
                )
    for l in range(TILES_DEV):
        cols = slice(TILE * l, TILE * l + TILE)
        total = lax.dot_general(
            steer_ref[...], rows_ref[:, cols], NN, preferred_element_type=jnp.float32
        )
        image_ref[:, cols] = total
        real, imag = total[:TILE], total[TILE:]
        power = real * real + imag * imag
        weight_ref[:TILE, cols] = (-power * imag).astype(jnp.bfloat16)
        weight_ref[TILE:, cols] = (power * real).astype(jnp.bfloat16)
    sums = []
    for h in range(KDIM // TILE):
        cols = slice(TILE * h, TILE * h + TILE)
        back = lax.dot_general(
            weight_ref[...], rows_ref[cols, :], NT, preferred_element_type=jnp.float32
        )
        sums.append(
            jnp.sum(back * steer_ref[:, cols].astype(jnp.float32), axis=0, keepdims=True)
        )
    halves = [-4.0 * (sums[h] + sums[h + 2]) for h in range(2)]
    for c in range(PULSES // LANE):
        piece = halves[c // 2][:, LANE * (c % 2) : LANE * (c % 2) + LANE]
        for b in range(N_BAND):
            grad_ref[b, c : c + 1, :] = piece


def image_kernel(flat_ref, out_ref):
    for comp in range(2):
        out_ref[comp, 0] = flat_ref[TILE * comp : TILE * comp + TILE, :].T


def spread_kernel(bands_ref, out_ref):
    total = jnp.sum(bands_ref[...], axis=0)
    for m in range(N_PULSE):
        out_ref[m] = total


def final_kernel(parts_ref, out_ref):
    me = lax.axis_index("pulse")
    gradient = jnp.sum(parts_ref[...], axis=0)
    square = jnp.sum(jnp.sum(gradient * gradient, axis=0, keepdims=True), axis=1, keepdims=True)
    scaled = gradient / jnp.sqrt(square / PULSES + 1e-05)
    row = lax.broadcasted_iota(jnp.int32, scaled.shape, 0)
    own = jnp.sum(jnp.where(row == me >> 3, scaled, 0.0), axis=0, keepdims=True)
    turned = pltpu.roll(jnp.broadcast_to(own, (8, LANE)), (LANE - P_DEV * (me & 7)) & (LANE - 1), 1)
    out_ref[...] = turned[:1, :P_DEV]


def kernel(body, name, out_shape, scratch=(), cost=None, **extra):
    return pl.pallas_call(
        body,
        out_shape=out_shape,
        scratch_shapes=list(scratch),
        compiler_params=pltpu.CompilerParams(vmem_limit_bytes=VMEM_BYTES),
        cost_estimate=pl.CostEstimate(flops=0, bytes_accessed=cost, transcendentals=0) if cost else None,
        name=name,
        **extra,
    )


def on_device(echoes, replica, pulse_angles, footprint, tile_slot, offsets):
    bf16, f32, i32 = jnp.bfloat16, jnp.float32, jnp.int32
    shape = jax.ShapeDtypeStruct
    window = pltpu.VMEM((ROWS + P_DEV * (SPANS - 1), 3 * TILE), bf16)
    tail = lax.ppermute(echoes, "band", [(i, i - 1) for i in range(1, N_BAND)])
    taps = kernel(
        taps_kernel, "taps", shape((TILE, 2 * TILE * SPANS), bf16), cost=8 << 20
    )(replica)
    steer, slots, local, hot, shift, turn, near = kernel(
        prep_kernel,
        "prep",
        [
            shape((2 * TILE, KDIM), bf16),
            shape((N_PULSE, LANE), i32),
            shape((N_PULSE, LANE), i32),
            shape((ROWS, ROWS), bf16),
            shape((ROWS // 2, LANE), i32),
            shape((2, ROWS // 2, LANE), f32),
            shape((2, ROWS, TILE), f32),
        ],
        scratch=[window, pltpu.VMEM((LANE, FOOT), i32)],
        cost=12 << 20,
    )(taps, echoes, pulse_angles, footprint.T, tile_slot.reshape(1, NTILE), offsets.T)
    rows = kernel(
        rows_kernel,
        "rows",
        shape((N_PULSE, 2, P_DEV, TILE), bf16),
        scratch=[window, pltpu.VMEM((2, (SPANS - 1) * P_DEV, TILE), f32)],
    )(tail, taps, near, hot, shift, turn, slots)
    arrived = lax.all_to_all(rows, "pulse", split_axis=0, concat_axis=0, tiled=True)
    image_flat, grad = kernel(
        owner_kernel,
        "owner",
        [
            shape((2 * TILE, TILES_DEV * TILE), f32),
            shape((N_BAND, PULSES // LANE, LANE), f32),
        ],
        scratch=[
            pltpu.VMEM((KDIM, TILES_DEV * TILE), bf16),
            pltpu.VMEM((2 * TILE, TILES_DEV * TILE), bf16),
        ],
    )(local, arrived, steer)
    image = kernel(
        image_kernel,
        "image",
        shape((2, TILES_DEV, TILE, TILE), f32),
        grid=(TILES_DEV,),
        in_specs=[pl.BlockSpec((2 * TILE, TILE), lambda l: (0, l))],
        out_specs=pl.BlockSpec((2, 1, TILE, TILE), lambda l: (0, l, 0, 0)),
    )(image_flat)
    bands = lax.all_to_all(grad, "band", split_axis=0, concat_axis=0, tiled=True)
    spread = kernel(spread_kernel, "spread", shape((N_PULSE, PULSES // LANE, LANE), f32))(bands)
    parts = lax.all_to_all(spread, "pulse", split_axis=0, concat_axis=0, tiled=True)
    own = kernel(final_kernel, "final", shape((1, P_DEV), f32))(parts)
    return (image, own.reshape(P_DEV))


def solution(mesh):
    placed = (P(None, "pulse", "band"), P(), P(), P(), P(), P())
    return jax.shard_map(
        on_device,
        mesh=mesh,
        in_specs=placed,
        out_specs=(P(None, "pulse", "band", None), P("pulse")),
        check_vma=False,
    )
```

```python
import math

import jax
import jax.numpy as jnp
from jax import lax
from jax.experimental import pallas as pl
from jax.experimental.pallas import tpu as pltpu
from jax.sharding import PartitionSpec as P

TILE = 256
TAPS = 2048
RB = 4096
P_DEV = 16
FOOT = 8
TILES_DEV = 4
NTILE = 128
PULSES = 512
N_PULSE = 32
N_BAND = 8
LANE = 128

SPANS = TAPS // TILE + 1
BLOCKS = RB // TILE
ROWS = BLOCKS * P_DEV
KDIM = 2 * PULSES
FACTOR = 0.5 / math.sqrt(P_DEV)

NT = (((1,), (1,)), ((), ()))
NN = (((1,), (0,)), ((), ()))

VMEM_BYTES = 24 * 1024 * 1024


def taps_kernel(replica_ref, taps_ref):
    width = TAPS + LANE
    chunks = width // LANE
    zero = jnp.zeros((16, LANE), jnp.bfloat16)
    for comp in range(2):
        line = replica_ref[comp : comp + 1, :].astype(jnp.float32)
        line = jnp.concatenate([line, jnp.zeros((1, LANE), jnp.float32)], axis=1)
        wide = jnp.broadcast_to(line, (8, width))
        base = pltpu.roll(wide, 0, 1, stride=1, stride_axis=0)
        for j in range(8):
            first = base if j == 0 else pltpu.roll(base, 16 * j, 1)
            pair = jnp.concatenate([first, pltpu.roll(base, 16 * j + 8, 1)], axis=0)
            pair = pair.astype(jnp.bfloat16)
            for half in range(2):
                row = LANE * half + 16 * j
                for c in range(2 * SPANS):
                    src = c - half
                    piece = pair[:, LANE * src : LANE * src + LANE] if 0 <= src < chunks else zero
                    col = 512 * (c // 2) + TILE * comp + LANE * (c % 2)
                    taps_ref[row : row + 16, col : col + LANE] = piece


def fill_steer(angle_ref, steer_ref):
    step = lax.broadcasted_iota(jnp.int32, (16, PULSES), 0).astype(jnp.float32)
    omega = angle_ref[0:1, :]
    fine, coarse = step * omega, (16.0 * step) * omega
    fine_cos, fine_sin = jnp.cos(fine), jnp.sin(fine)
    coarse_cos, coarse_sin = jnp.cos(coarse), jnp.sin(coarse)
    for a in range(TILE // 16):
        ca, sa = coarse_cos[a : a + 1], coarse_sin[a : a + 1]
        cosine = (fine_cos * ca - fine_sin * sa).astype(jnp.bfloat16)
        sine = (fine_sin * ca + fine_cos * sa).astype(jnp.bfloat16)
        upper, lower = slice(16 * a, 16 * a + 16), slice(TILE + 16 * a, TILE + 16 * a + 16)
        steer_ref[upper, :PULSES] = cosine
        steer_ref[upper, PULSES:] = -sine
        steer_ref[lower, :PULSES] = sine
        steer_ref[lower, PULSES:] = cosine


def own_lanes():
    lane = lax.broadcasted_iota(jnp.int32, (P_DEV, PULSES), 1)
    sub = lax.broadcasted_iota(jnp.int32, (P_DEV, PULSES), 0)
    return lane == lax.axis_index("pulse") * P_DEV + sub


def prep_kernel(
    taps_ref,
    echo_ref,
    angle_ref,
    footprint_ref,
    slot_ref,
    offset_ref,
    steer_ref,
    slots_ref,
    local_ref,
    hot_ref,
    shift_ref,
    turn_ref,
    near_ref,
    win_ref,
    listed_ref,
):
    me = lax.axis_index("pulse")
    fill_steer(angle_ref, steer_ref)

    for n in range(BLOCKS):
        rows = slice(P_DEV * n, P_DEV * n + P_DEV)
        real = echo_ref[0, :, TILE * n : TILE * n + TILE]
        win_ref[rows, :TILE] = real
        win_ref[rows, TILE : 2 * TILE] = echo_ref[1, :, TILE * n : TILE * n + TILE]
        win_ref[rows, 2 * TILE :] = -real
    win_ref[ROWS:, :] = jnp.zeros((P_DEV * (SPANS - 1), 3 * TILE), jnp.bfloat16)
    correlate(win_ref, taps_ref, near_ref, 0, 0, None)

    listed = jnp.concatenate([footprint_ref[...], jnp.full((FOOT, LANE - N_PULSE), -1)], axis=1)
    listed = listed.T
    listed_ref[...] = listed
    lane = lax.broadcasted_iota(jnp.int32, (N_PULSE, LANE), 1)
    slots = jnp.zeros((N_PULSE, LANE), jnp.int32)
    local = jnp.zeros((N_PULSE, 1), jnp.int32)
    for k in range(FOOT):
        same = listed[:N_PULSE, k : k + 1] == lane
        slot = jnp.sum(jnp.where(same, slot_ref[...] + 1, 0), axis=1, keepdims=True)
        slots = jnp.where(lane == k, slot, slots)
        owned = (slot > 0) & (((slot - 1) >> 2) == me)
        local = jnp.where(owned, ((slot - 1) & 3) + 1, local)
    slots_ref[...] = slots
    local_ref[...] = jnp.broadcast_to(local, (N_PULSE, LANE))

    mine = own_lanes()
    tiles = jnp.maximum(listed_ref[pl.ds(me, 1), :], 0).astype(jnp.float32)
    kappa = jnp.sum(jnp.where(mine, angle_ref[1:2, :], 0.0), axis=1, keepdims=True)
    phase = jnp.sum(jnp.where(mine, angle_ref[2:3, :], 0.0), axis=1, keepdims=True)
    turn = kappa * tiles + phase
    cosine, sine = jnp.cos(turn), jnp.sin(turn)
    pulse = lax.broadcasted_iota(jnp.int32, (P_DEV, ROWS), 0)
    pick = lax.broadcasted_iota(jnp.int32, (P_DEV, ROWS), 1)
    low_hot, high_hot = [], []
    for k in range(FOOT):
        rows = slice(P_DEV * k, P_DEV * k + P_DEV)
        offset = jnp.sum(jnp.where(mine, offset_ref[k : k + 1, :], 0), axis=1, keepdims=True)
        block = offset >> 8
        low_hot.append(jnp.where(pick == block * P_DEV + pulse, 1.0, 0.0))
        block = jnp.minimum(block + 1, BLOCKS - 1)
        high_hot.append(jnp.where(pick == block * P_DEV + pulse, 1.0, 0.0))
        shift_ref[rows, :] = jnp.broadcast_to(offset & (TILE - 1), (P_DEV, LANE))
        turn_ref[0, rows, :] = jnp.broadcast_to(cosine[:, k : k + 1], (P_DEV, LANE))
        turn_ref[1, rows, :] = jnp.broadcast_to(sine[:, k : k + 1], (P_DEV, LANE))
    hot_ref[...] = jnp.concatenate(low_hot + high_hot, axis=0).astype(jnp.bfloat16)


def correlate(win_ref, taps_ref, out_ref, first_row, first_span, add_ref):
    count = out_ref.shape[1]
    left = []
    for comp in range(2):
        cols = slice(TILE * comp, TILE * comp + 2 * TILE)
        spans = [
            win_ref[first_row + P_DEV * a : first_row + P_DEV * a + count, cols]
            for a in range(first_span, SPANS)
        ]
        left.append(jnp.concatenate(spans, axis=1))
    total = lax.dot_general(
        jnp.concatenate(left, axis=0),
        taps_ref[:, 2 * TILE * first_span :],
        NT,
        preferred_element_type=jnp.float32,
    )
    for comp in range(2):
        part = total[count * comp : count * comp + count]
        out_ref[comp] = part if add_ref is None else part + add_ref[comp, first_row:, :]


def lane_shift(low, high, shift):
    first, second = low[:, :LANE], low[:, LANE:]
    third, fourth = high[:, :LANE], high[:, LANE:]
    far = shift >= LANE
    parts = [
        jnp.where(far, second, first),
        jnp.where(far, third, second),
        jnp.where(far, fourth, third),
    ]
    step = shift & (LANE - 1)
    lane = lax.broadcasted_iota(jnp.int32, first.shape, 1)
    index = (lane + step) & (LANE - 1)
    turned = [jnp.take_along_axis(part, index, axis=1) for part in parts]
    stay = lane < LANE - step
    return jnp.concatenate(
        [jnp.where(stay, turned[0], turned[1]), jnp.where(stay, turned[1], turned[2])], axis=1
    )


def rows_kernel(
    tail_ref,
    taps_ref,
    near_ref,
    hot_ref,
    shift_ref,
    turn_ref,
    slots_ref,
    out_ref,
    win_ref,
    far_ref,
):
    me = lax.axis_index("pulse")
    half = (BLOCKS - SPANS + 1) * P_DEV
    win_ref[:ROWS, :] = jnp.zeros((ROWS, 3 * TILE), jnp.bfloat16)
    for n in range(SPANS - 1):
        rows = slice(ROWS + P_DEV * n, ROWS + P_DEV * n + P_DEV)
        real = tail_ref[0, :, TILE * n : TILE * n + TILE]
        win_ref[rows, :TILE] = real
        win_ref[rows, TILE : 2 * TILE] = tail_ref[1, :, TILE * n : TILE * n + TILE]
        win_ref[rows, 2 * TILE :] = -real
    correlate(win_ref, taps_ref, far_ref, half, 1, near_ref)
    series = jnp.concatenate(
        [
            jnp.concatenate([near_ref[0, :half, :], near_ref[1, :half, :]], axis=1),
            jnp.concatenate([far_ref[0], far_ref[1]], axis=1),
        ],
        axis=0,
    ).astype(jnp.bfloat16)
    picked = lax.dot_general(hot_ref[...], series, NN, preferred_element_type=jnp.float32)
    out_ref[...] = jnp.zeros_like(out_ref)
    for k in reversed(range(FOOT)):
        rows = slice(P_DEV * k, P_DEV * k + P_DEV)
        low = picked[P_DEV * k : P_DEV * k + P_DEV]
        high = picked[P_DEV * (FOOT + k) : P_DEV * (FOOT + k) + P_DEV]
        shift = shift_ref[rows, :]
        real = lane_shift(low[:, :TILE], high[:, :TILE], shift)
        imag = lane_shift(low[:, TILE:], high[:, TILE:], shift)
        c = jnp.concatenate([turn_ref[0, rows, :]] * 2, axis=1)
        s = jnp.concatenate([turn_ref[1, rows, :]] * 2, axis=1)
        slot = slots_ref[me, k]
        owner = (jnp.where(slot > 0, slot, slots_ref[me, 0]) - 1) >> 2
        out_ref[owner, 0] = ((real * c - imag * s) * FACTOR).astype(jnp.bfloat16)
        out_ref[owner, 1] = ((real * s + imag * c) * FACTOR).astype(jnp.bfloat16)


def owner_kernel(
    local_ref,
    arrived_ref,
    steer_ref,
    image_hbm,
    grad_ref,
    rows_ref,
    weight_ref,
    flat_ref,
    image_ref,
    image_sem,
):
    for d in range(N_PULSE):
        slot = local_ref[d, 0]
        for comp in range(2):
            piece = arrived_ref[d, comp]
            row = PULSES * comp + P_DEV * d
            for l in range(TILES_DEV):
                rows_ref[row : row + P_DEV, TILE * l : TILE * l + TILE] = jnp.where(
                    slot == l + 1, piece, jnp.zeros_like(piece)
                )
    copies, sums = [], []

    def write_out(l):
        cols = slice(TILE * l, TILE * l + TILE)
        for c in range(2):
            image_ref[l, c] = flat_ref[TILE * c : TILE * c + TILE, cols].T
            copy = pltpu.make_async_copy(image_ref.at[l, c], image_hbm.at[c, l], image_sem.at[l, c])
            copy.start()
            copies.append(copy)

    for l in range(TILES_DEV):
        cols = slice(TILE * l, TILE * l + TILE)
        total = lax.dot_general(
            steer_ref[...], rows_ref[:, cols], NN, preferred_element_type=jnp.float32
        )
        flat_ref[:, cols] = total
        if l > 0:
            write_out(l - 1)
        real, imag = total[:TILE], total[TILE:]
        power = real * real + imag * imag
        weight_ref[:TILE, cols] = (-power * imag).astype(jnp.bfloat16)
        weight_ref[TILE:, cols] = (power * real).astype(jnp.bfloat16)
    for h in range(KDIM // TILE):
        cols = slice(TILE * h, TILE * h + TILE)
        back = lax.dot_general(
            weight_ref[...], rows_ref[cols, :], NT, preferred_element_type=jnp.float32
        )
        if h == 0:
            write_out(TILES_DEV - 1)
        sums.append(
            jnp.sum(back * steer_ref[:, cols].astype(jnp.float32), axis=0, keepdims=True)
        )
    halves = [-4.0 * (sums[h] + sums[h + 2]) for h in range(2)]
    for c in range(PULSES // LANE):
        grad_ref[c : c + 1, :] = halves[c // 2][:, LANE * (c % 2) : LANE * (c % 2) + LANE]
    for copy in copies:
        copy.wait()


def spread_kernel(own_ref, other_ref, out_ref):
    total = (own_ref[...] + other_ref[...]).astype(jnp.bfloat16)
    for m in range(N_PULSE * N_BAND // 2):
        out_ref[m] = total


def final_kernel(parts_ref, out_ref):
    me = lax.axis_index("pulse")
    gradient = jnp.sum(parts_ref[...].astype(jnp.float32), axis=0)
    square = jnp.sum(jnp.sum(gradient * gradient, axis=0, keepdims=True), axis=1, keepdims=True)
    scaled = gradient / jnp.sqrt(square / PULSES + 1e-05)
    row = lax.broadcasted_iota(jnp.int32, scaled.shape, 0)
    own = jnp.sum(jnp.where(row == me >> 3, scaled, 0.0), axis=0, keepdims=True)
    turned = pltpu.roll(jnp.broadcast_to(own, (8, LANE)), (LANE - P_DEV * (me & 7)) & (LANE - 1), 1)
    out_ref[...] = turned[:1, :P_DEV]


def kernel(body, name, out_shape, scratch=(), cost=None, **extra):
    return pl.pallas_call(
        body,
        out_shape=out_shape,
        scratch_shapes=list(scratch),
        compiler_params=pltpu.CompilerParams(vmem_limit_bytes=VMEM_BYTES),
        cost_estimate=pl.CostEstimate(flops=0, bytes_accessed=cost, transcendentals=0) if cost else None,
        name=name,
        **extra,
    )


def on_device(echoes, replica, pulse_angles, footprint, tile_slot, offsets):
    bf16, f32, i32 = jnp.bfloat16, jnp.float32, jnp.int32
    shape = jax.ShapeDtypeStruct
    window = pltpu.VMEM((ROWS + P_DEV * (SPANS - 1), 3 * TILE), bf16)
    tail = lax.ppermute(echoes, "band", [(i, i - 1) for i in range(1, N_BAND)])
    taps = kernel(
        taps_kernel, "taps", shape((TILE, 2 * TILE * SPANS), bf16), cost=8 << 20
    )(replica)
    steer, slots, local, hot, shift, turn, near = kernel(
        prep_kernel,
        "prep",
        [
            shape((2 * TILE, KDIM), bf16),
            shape((N_PULSE, LANE), i32),
            shape((N_PULSE, LANE), i32),
            shape((ROWS, ROWS), bf16),
            shape((ROWS // 2, LANE), i32),
            shape((2, ROWS // 2, LANE), f32),
            shape((2, ROWS, TILE), f32),
        ],
        scratch=[window, pltpu.VMEM((LANE, FOOT), i32)],
        cost=12 << 20,
    )(taps, echoes, pulse_angles, footprint.T, tile_slot.reshape(1, NTILE), offsets.T)
    rows = kernel(
        rows_kernel,
        "rows",
        shape((N_PULSE, 2, P_DEV, TILE), bf16),
        scratch=[window, pltpu.VMEM((2, (SPANS - 1) * P_DEV, TILE), f32)],
    )(tail, taps, near, hot, shift, turn, slots)
    arrived = lax.all_to_all(rows, "pulse", split_axis=0, concat_axis=0, tiled=True)
    image, grad = kernel(
        owner_kernel,
        "owner",
        [
            shape((2, TILES_DEV, TILE, TILE), f32),
            shape((PULSES // LANE, LANE), f32),
        ],
        out_specs=[pl.BlockSpec(memory_space=pl.ANY), pl.BlockSpec(memory_space=pltpu.VMEM)],
        scratch=[
            pltpu.VMEM((KDIM, TILES_DEV * TILE), bf16),
            pltpu.VMEM((2 * TILE, TILES_DEV * TILE), bf16),
            pltpu.VMEM((2 * TILE, TILES_DEV * TILE), f32),
            pltpu.VMEM((TILES_DEV, 2, TILE, TILE), f32),
            pltpu.SemaphoreType.DMA((TILES_DEV, 2)),
        ],
    )(local, arrived, steer)
    other = lax.ppermute(grad, "band", [(i, i ^ 1) for i in range(N_BAND)])
    chips = N_PULSE * N_BAND // 2
    spread = kernel(spread_kernel, "spread", shape((chips, PULSES // LANE, LANE), bf16))(
        grad, other
    )
    parts = lax.all_to_all(
        spread,
        ("pulse", "band"),
        split_axis=0,
        concat_axis=0,
        axis_index_groups=[list(range(core, 2 * chips, 2)) for core in range(2)],
        tiled=True,
    )
    own = kernel(final_kernel, "final", shape((1, P_DEV), f32))(parts)
    return (image, own.reshape(P_DEV))


def solution(mesh):
    placed = (P(None, "pulse", "band"), P(), P(), P(), P(), P())
    return jax.shard_map(
        on_device,
        mesh=mesh,
        in_specs=placed,
        out_specs=(P(None, "pulse", "band", None), P("pulse")),
        check_vma=False,
    )
```

```python
import math

import jax
import jax.numpy as jnp
from jax import lax
from jax.experimental import pallas as pl
from jax.experimental.pallas import tpu as pltpu
from jax.sharding import PartitionSpec as P

TILE = 256
TAPS = 2048
RB = 4096
P_DEV = 16
FOOT = 8
TILES_DEV = 4
NTILE = 128
PULSES = 512
N_PULSE = 32
N_BAND = 8
LANE = 128

SPANS = TAPS // TILE + 1
BLOCKS = RB // TILE
ROWS = BLOCKS * P_DEV
KDIM = 2 * PULSES
FACTOR = 0.5 / math.sqrt(P_DEV)

NT = (((1,), (1,)), ((), ()))
NN = (((1,), (0,)), ((), ()))

VMEM_BYTES = 24 * 1024 * 1024


def taps_kernel(replica_ref, taps_ref):
    width = TAPS + LANE
    chunks = width // LANE
    zero = jnp.zeros((16, LANE), jnp.bfloat16)
    for comp in range(2):
        line = replica_ref[comp : comp + 1, :].astype(jnp.float32)
        line = jnp.concatenate([line, jnp.zeros((1, LANE), jnp.float32)], axis=1)
        wide = jnp.broadcast_to(line, (8, width))
        base = pltpu.roll(wide, 0, 1, stride=1, stride_axis=0)
        for j in range(8):
            first = base if j == 0 else pltpu.roll(base, 16 * j, 1)
            pair = jnp.concatenate([first, pltpu.roll(base, 16 * j + 8, 1)], axis=0)
            pair = pair.astype(jnp.bfloat16)
            for half in range(2):
                row = LANE * half + 16 * j
                for c in range(2 * SPANS):
                    src = c - half
                    piece = pair[:, LANE * src : LANE * src + LANE] if 0 <= src < chunks else zero
                    col = 512 * (c // 2) + TILE * comp + LANE * (c % 2)
                    taps_ref[row : row + 16, col : col + LANE] = piece


def fill_steer(angle_ref, steer_ref):
    step = lax.broadcasted_iota(jnp.int32, (16, PULSES), 0).astype(jnp.float32)
    omega = angle_ref[0:1, :]
    fine, coarse = step * omega, (16.0 * step) * omega
    fine_cos, fine_sin = jnp.cos(fine), jnp.sin(fine)
    coarse_cos, coarse_sin = jnp.cos(coarse), jnp.sin(coarse)
    for a in range(TILE // 16):
        ca, sa = coarse_cos[a : a + 1], coarse_sin[a : a + 1]
        cosine = (fine_cos * ca - fine_sin * sa).astype(jnp.bfloat16)
        sine = (fine_sin * ca + fine_cos * sa).astype(jnp.bfloat16)
        upper, lower = slice(16 * a, 16 * a + 16), slice(TILE + 16 * a, TILE + 16 * a + 16)
        steer_ref[upper, :PULSES] = cosine
        steer_ref[upper, PULSES:] = -sine
        steer_ref[lower, :PULSES] = sine
        steer_ref[lower, PULSES:] = cosine


def own_lanes():
    lane = lax.broadcasted_iota(jnp.int32, (P_DEV, PULSES), 1)
    sub = lax.broadcasted_iota(jnp.int32, (P_DEV, PULSES), 0)
    return lane == lax.axis_index("pulse") * P_DEV + sub


def prep_kernel(
    taps_ref,
    echo_ref,
    angle_ref,
    footprint_ref,
    slot_ref,
    offset_ref,
    steer_ref,
    slots_ref,
    local_ref,
    hot_ref,
    shift_ref,
    turn_ref,
    near_ref,
    win_ref,
    listed_ref,
):
    me = lax.axis_index("pulse")
    fill_steer(angle_ref, steer_ref)

    for n in range(BLOCKS):
        rows = slice(P_DEV * n, P_DEV * n + P_DEV)
        real = echo_ref[0, :, TILE * n : TILE * n + TILE]
        win_ref[rows, :TILE] = real
        win_ref[rows, TILE : 2 * TILE] = echo_ref[1, :, TILE * n : TILE * n + TILE]
        win_ref[rows, 2 * TILE :] = -real
    win_ref[ROWS:, :] = jnp.zeros((P_DEV * (SPANS - 1), 3 * TILE), jnp.bfloat16)
    correlate(win_ref, taps_ref, near_ref, 0, 0, None)

    listed = jnp.concatenate([footprint_ref[...], jnp.full((FOOT, LANE - N_PULSE), -1)], axis=1)
    listed = listed.T
    listed_ref[...] = listed
    places = (slot_ref[...] + 1).astype(jnp.float32)
    lane = lax.broadcasted_iota(jnp.int32, (N_PULSE, LANE), 1)
    slots = jnp.zeros((N_PULSE, LANE), jnp.int32)
    local = jnp.zeros((N_PULSE, 1), jnp.int32)
    for k in range(FOOT):
        same = listed[:N_PULSE, k : k + 1] == lane
        slot = jnp.sum(jnp.where(same, places, 0.0), axis=1, keepdims=True).astype(jnp.int32)
        slots = jnp.where(lane == k, slot, slots)
        owned = (slot > 0) & (((slot - 1) >> 2) == me)
        local = jnp.where(owned, ((slot - 1) & 3) + 1, local)
    slots_ref[...] = slots
    local_ref[...] = jnp.broadcast_to(local, (N_PULSE, LANE))

    mine = own_lanes()
    tiles = jnp.maximum(listed_ref[pl.ds(me, 1), :], 0).astype(jnp.float32)
    kappa = jnp.sum(jnp.where(mine, angle_ref[1:2, :], 0.0), axis=1, keepdims=True)
    phase = jnp.sum(jnp.where(mine, angle_ref[2:3, :], 0.0), axis=1, keepdims=True)
    turn = kappa * tiles + phase
    cosine, sine = jnp.cos(turn), jnp.sin(turn)
    pulse = lax.broadcasted_iota(jnp.int32, (P_DEV, ROWS), 0)
    pick = lax.broadcasted_iota(jnp.int32, (P_DEV, ROWS), 1)
    low_hot, high_hot = [], []
    for k in range(FOOT):
        rows = slice(P_DEV * k, P_DEV * k + P_DEV)
        offset = offset_ref[k : k + 1, :].astype(jnp.float32)
        offset = jnp.sum(jnp.where(mine, offset, 0.0), axis=1, keepdims=True).astype(jnp.int32)
        block = offset >> 8
        low_hot.append(jnp.where(pick == block * P_DEV + pulse, 1.0, 0.0))
        block = jnp.minimum(block + 1, BLOCKS - 1)
        high_hot.append(jnp.where(pick == block * P_DEV + pulse, 1.0, 0.0))
        shift_ref[rows, :] = jnp.broadcast_to(offset & (TILE - 1), (P_DEV, LANE))
        turn_ref[0, rows, :] = jnp.broadcast_to(cosine[:, k : k + 1], (P_DEV, LANE))
        turn_ref[1, rows, :] = jnp.broadcast_to(sine[:, k : k + 1], (P_DEV, LANE))
    hot_ref[...] = jnp.concatenate(low_hot + high_hot, axis=0).astype(jnp.bfloat16)


def correlate(win_ref, taps_ref, out_ref, first_row, first_span, add_ref):
    count = out_ref.shape[1]
    left = []
    for comp in range(2):
        cols = slice(TILE * comp, TILE * comp + 2 * TILE)
        spans = [
            win_ref[first_row + P_DEV * a : first_row + P_DEV * a + count, cols]
            for a in range(first_span, SPANS)
        ]
        left.append(jnp.concatenate(spans, axis=1))
    total = lax.dot_general(
        jnp.concatenate(left, axis=0),
        taps_ref[:, 2 * TILE * first_span :],
        NT,
        preferred_element_type=jnp.float32,
    )
    for comp in range(2):
        part = total[count * comp : count * comp + count]
        out_ref[comp] = part if add_ref is None else part + add_ref[comp, first_row:, :]


def lane_shift(low, high, shift):
    first, second = low[:, :LANE], low[:, LANE:]
    third, fourth = high[:, :LANE], high[:, LANE:]
    far = shift >= LANE
    parts = [
        jnp.where(far, second, first),
        jnp.where(far, third, second),
        jnp.where(far, fourth, third),
    ]
    step = shift & (LANE - 1)
    lane = lax.broadcasted_iota(jnp.int32, first.shape, 1)
    index = (lane + step) & (LANE - 1)
    turned = [jnp.take_along_axis(part, index, axis=1) for part in parts]
    stay = lane < LANE - step
    return jnp.concatenate(
        [jnp.where(stay, turned[0], turned[1]), jnp.where(stay, turned[1], turned[2])], axis=1
    )


def rows_kernel(
    tail_ref,
    taps_ref,
    near_ref,
    hot_ref,
    shift_ref,
    turn_ref,
    slots_ref,
    out_ref,
    win_ref,
    far_ref,
):
    me = lax.axis_index("pulse")
    half = (BLOCKS - SPANS + 1) * P_DEV
    win_ref[:ROWS, :] = jnp.zeros((ROWS, 3 * TILE), jnp.bfloat16)
    for n in range(SPANS - 1):
        rows = slice(ROWS + P_DEV * n, ROWS + P_DEV * n + P_DEV)
        real = tail_ref[0, :, TILE * n : TILE * n + TILE]
        win_ref[rows, :TILE] = real
        win_ref[rows, TILE : 2 * TILE] = tail_ref[1, :, TILE * n : TILE * n + TILE]
        win_ref[rows, 2 * TILE :] = -real
    correlate(win_ref, taps_ref, far_ref, half, 1, near_ref)
    series = jnp.concatenate(
        [
            jnp.concatenate([near_ref[0, :half, :], near_ref[1, :half, :]], axis=1),
            jnp.concatenate([far_ref[0], far_ref[1]], axis=1),
        ],
        axis=0,
    ).astype(jnp.bfloat16)
    picked = lax.dot_general(hot_ref[...], series, NN, preferred_element_type=jnp.float32)
    out_ref[...] = jnp.zeros_like(out_ref)
    for k in reversed(range(FOOT)):
        rows = slice(P_DEV * k, P_DEV * k + P_DEV)
        low = picked[P_DEV * k : P_DEV * k + P_DEV]
        high = picked[P_DEV * (FOOT + k) : P_DEV * (FOOT + k) + P_DEV]
        shift = shift_ref[rows, :]
        real = lane_shift(low[:, :TILE], high[:, :TILE], shift)
        imag = lane_shift(low[:, TILE:], high[:, TILE:], shift)
        c = jnp.concatenate([turn_ref[0, rows, :]] * 2, axis=1)
        s = jnp.concatenate([turn_ref[1, rows, :]] * 2, axis=1)
        slot = slots_ref[me, k]
        owner = (jnp.where(slot > 0, slot, slots_ref[me, 0]) - 1) >> 2
        out_ref[owner, 0] = ((real * c - imag * s) * FACTOR).astype(jnp.bfloat16)
        out_ref[owner, 1] = ((real * s + imag * c) * FACTOR).astype(jnp.bfloat16)


def owner_kernel(
    local_ref,
    arrived_ref,
    steer_ref,
    image_hbm,
    grad_ref,
    rows_ref,
    weight_ref,
    flat_ref,
    image_ref,
    image_sem,
):
    for d in range(N_PULSE):
        slot = local_ref[d, 0]
        for comp in range(2):
            piece = arrived_ref[d, comp]
            row = PULSES * comp + P_DEV * d
            for l in range(TILES_DEV):
                rows_ref[row : row + P_DEV, TILE * l : TILE * l + TILE] = jnp.where(
                    slot == l + 1, piece, jnp.zeros_like(piece)
                )
    copies, sums = [], []

    def write_out(l):
        cols = slice(TILE * l, TILE * l + TILE)
        for c in range(2):
            image_ref[l, c] = flat_ref[TILE * c : TILE * c + TILE, cols].T
            copy = pltpu.make_async_copy(image_ref.at[l, c], image_hbm.at[c, l], image_sem.at[l, c])
            copy.start()
            copies.append(copy)

    for l in range(TILES_DEV):
        cols = slice(TILE * l, TILE * l + TILE)
        total = lax.dot_general(
            steer_ref[...], rows_ref[:, cols], NN, preferred_element_type=jnp.float32
        )
        flat_ref[:, cols] = total
        if l > 0:
            write_out(l - 1)
        real, imag = total[:TILE], total[TILE:]
        power = real * real + imag * imag
        weight_ref[:TILE, cols] = (-power * imag).astype(jnp.bfloat16)
        weight_ref[TILE:, cols] = (power * real).astype(jnp.bfloat16)
    for h in range(KDIM // TILE):
        cols = slice(TILE * h, TILE * h + TILE)
        back = lax.dot_general(
            weight_ref[...], rows_ref[cols, :], NT, preferred_element_type=jnp.float32
        )
        if h == 0:
            write_out(TILES_DEV - 1)
        sums.append(
            jnp.sum(back * steer_ref[:, cols].astype(jnp.float32), axis=0, keepdims=True)
        )
    halves = [-4.0 * (sums[h] + sums[h + 2]) for h in range(2)]
    for c in range(PULSES // LANE):
        grad_ref[c : c + 1, :] = halves[c // 2][:, LANE * (c % 2) : LANE * (c % 2) + LANE]
    for copy in copies:
        copy.wait()


def spread_kernel(own_ref, other_ref, out_ref):
    total = (own_ref[...] + other_ref[...]).astype(jnp.bfloat16)
    for m in range(N_PULSE * N_BAND // 2):
        out_ref[m] = total


def final_kernel(parts_ref, out_ref):
    me = lax.axis_index("pulse")
    gradient = jnp.sum(parts_ref[...].astype(jnp.float32), axis=0)
    square = jnp.sum(jnp.sum(gradient * gradient, axis=0, keepdims=True), axis=1, keepdims=True)
    scaled = gradient / jnp.sqrt(square / PULSES + 1e-05)
    row = lax.broadcasted_iota(jnp.int32, scaled.shape, 0)
    own = jnp.sum(jnp.where(row == me >> 3, scaled, 0.0), axis=0, keepdims=True)
    turned = pltpu.roll(jnp.broadcast_to(own, (8, LANE)), (LANE - P_DEV * (me & 7)) & (LANE - 1), 1)
    out_ref[...] = turned[:1, :P_DEV]


def kernel(body, name, out_shape, scratch=(), cost=None, **extra):
    return pl.pallas_call(
        body,
        out_shape=out_shape,
        scratch_shapes=list(scratch),
        compiler_params=pltpu.CompilerParams(vmem_limit_bytes=VMEM_BYTES),
        cost_estimate=pl.CostEstimate(flops=0, bytes_accessed=cost, transcendentals=0) if cost else None,
        name=name,
        **extra,
    )


def on_device(echoes, replica, pulse_angles, footprint, tile_slot, offsets):
    bf16, f32, i32 = jnp.bfloat16, jnp.float32, jnp.int32
    shape = jax.ShapeDtypeStruct
    window = pltpu.VMEM((ROWS + P_DEV * (SPANS - 1), 3 * TILE), bf16)
    tail = lax.ppermute(echoes[:, :, :TAPS], "band", [(i, i - 1) for i in range(1, N_BAND)])
    taps = kernel(
        taps_kernel, "taps", shape((TILE, 2 * TILE * SPANS), bf16), cost=8 << 20
    )(replica)
    steer, slots, local, hot, shift, turn, near = kernel(
        prep_kernel,
        "prep",
        [
            shape((2 * TILE, KDIM), bf16),
            shape((N_PULSE, LANE), i32),
            shape((N_PULSE, LANE), i32),
            shape((ROWS, ROWS), bf16),
            shape((ROWS // 2, LANE), i32),
            shape((2, ROWS // 2, LANE), f32),
            shape((2, ROWS, TILE), f32),
        ],
        scratch=[window, pltpu.VMEM((LANE, FOOT), i32)],
        cost=12 << 20,
    )(taps, echoes, pulse_angles, footprint.T, tile_slot.reshape(1, NTILE), offsets.T)
    rows = kernel(
        rows_kernel,
        "rows",
        shape((N_PULSE, 2, P_DEV, TILE), bf16),
        scratch=[window, pltpu.VMEM((2, (SPANS - 1) * P_DEV, TILE), f32)],
    )(tail, taps, near, hot, shift, turn, slots)
    arrived = lax.all_to_all(rows, "pulse", split_axis=0, concat_axis=0, tiled=True)
    image, grad = kernel(
        owner_kernel,
        "owner",
        [
            shape((2, TILES_DEV, TILE, TILE), f32),
            shape((PULSES // LANE, LANE), f32),
        ],
        out_specs=[pl.BlockSpec(memory_space=pl.ANY), pl.BlockSpec(memory_space=pltpu.VMEM)],
        scratch=[
            pltpu.VMEM((KDIM, TILES_DEV * TILE), bf16),
            pltpu.VMEM((2 * TILE, TILES_DEV * TILE), bf16),
            pltpu.VMEM((2 * TILE, TILES_DEV * TILE), f32),
            pltpu.VMEM((TILES_DEV, 2, TILE, TILE), f32),
            pltpu.SemaphoreType.DMA((TILES_DEV, 2)),
        ],
    )(local, arrived, steer)
    other = lax.ppermute(grad, "band", [(i, i ^ 1) for i in range(N_BAND)])
    chips = N_PULSE * N_BAND // 2
    spread = kernel(spread_kernel, "spread", shape((chips, PULSES // LANE, LANE), bf16))(
        grad, other
    )
    parts = lax.all_to_all(
        spread,
        ("pulse", "band"),
        split_axis=0,
        concat_axis=0,
        axis_index_groups=[list(range(core, 2 * chips, 2)) for core in range(2)],
        tiled=True,
    )
    own = kernel(final_kernel, "final", shape((1, P_DEV), f32))(parts)
    return (image, own.reshape(P_DEV))


def solution(mesh):
    placed = (P(None, "pulse", "band"), P(), P(), P(), P(), P())
    return jax.shard_map(
        on_device,
        mesh=mesh,
        in_specs=placed,
        out_specs=(P(None, "pulse", "band", None), P("pulse")),
        check_vma=False,
    )
```

```python
import math

import jax
import jax.numpy as jnp
from jax import lax
from jax.experimental import pallas as pl
from jax.experimental.pallas import tpu as pltpu
from jax.sharding import PartitionSpec as P

TILE = 256
TAPS = 2048
RB = 4096
P_DEV = 16
FOOT = 8
TILES_DEV = 4
NTILE = 128
PULSES = 512
N_PULSE = 32
N_BAND = 8
LANE = 128

SPANS = TAPS // TILE + 1
BLOCKS = RB // TILE
ROWS = BLOCKS * P_DEV
KDIM = 2 * PULSES
FACTOR = 0.5 / math.sqrt(P_DEV)

NT = (((1,), (1,)), ((), ()))
NN = (((1,), (0,)), ((), ()))

VMEM_BYTES = 24 * 1024 * 1024


def taps_kernel(replica_ref, taps_ref):
    width = TAPS + LANE
    chunks = width // LANE
    zero = jnp.zeros((16, LANE), jnp.bfloat16)
    for comp in range(2):
        line = replica_ref[comp : comp + 1, :].astype(jnp.float32)
        line = jnp.concatenate([line, jnp.zeros((1, LANE), jnp.float32)], axis=1)
        wide = jnp.broadcast_to(line, (8, width))
        base = pltpu.roll(wide, 0, 1, stride=1, stride_axis=0)
        for j in range(8):
            first = base if j == 0 else pltpu.roll(base, 16 * j, 1)
            pair = jnp.concatenate([first, pltpu.roll(base, 16 * j + 8, 1)], axis=0)
            pair = pair.astype(jnp.bfloat16)
            for half in range(2):
                row = LANE * half + 16 * j
                for c in range(2 * SPANS):
                    src = c - half
                    piece = pair[:, LANE * src : LANE * src + LANE] if 0 <= src < chunks else zero
                    col = 512 * (c // 2) + TILE * comp + LANE * (c % 2)
                    taps_ref[row : row + 16, col : col + LANE] = piece


def fill_steer(fine_cos, fine_sin, steer_ref):
    coarse_cos, coarse_sin = fine_cos, fine_sin
    for _ in range(4):
        coarse_cos, coarse_sin = (
            coarse_cos * coarse_cos - coarse_sin * coarse_sin,
            2.0 * coarse_cos * coarse_sin,
        )
    for a in range(TILE // 16):
        ca, sa = coarse_cos[a : a + 1], coarse_sin[a : a + 1]
        cosine = (fine_cos * ca - fine_sin * sa).astype(jnp.bfloat16)
        sine = (fine_sin * ca + fine_cos * sa).astype(jnp.bfloat16)
        upper, lower = slice(16 * a, 16 * a + 16), slice(TILE + 16 * a, TILE + 16 * a + 16)
        steer_ref[upper, :PULSES] = cosine
        steer_ref[upper, PULSES:] = -sine
        steer_ref[lower, :PULSES] = sine
        steer_ref[lower, PULSES:] = cosine


def own_lanes():
    lane = lax.broadcasted_iota(jnp.int32, (P_DEV, PULSES), 1)
    sub = lax.broadcasted_iota(jnp.int32, (P_DEV, PULSES), 0)
    return lane == lax.axis_index("pulse") * P_DEV + sub


def prep_kernel(
    taps_ref,
    echo_ref,
    angle_ref,
    footprint_ref,
    slot_ref,
    offset_ref,
    steer_ref,
    slots_ref,
    local_ref,
    hot_ref,
    shift_ref,
    turn_ref,
    near_ref,
    win_ref,
    listed_ref,
):
    me = lax.axis_index("pulse")

    for n in range(BLOCKS):
        rows = slice(P_DEV * n, P_DEV * n + P_DEV)
        real = echo_ref[0, :, TILE * n : TILE * n + TILE]
        win_ref[rows, :TILE] = real
        win_ref[rows, TILE : 2 * TILE] = echo_ref[1, :, TILE * n : TILE * n + TILE]
        win_ref[rows, 2 * TILE :] = -real
    win_ref[ROWS:, :] = jnp.zeros((P_DEV * (SPANS - 1), 3 * TILE), jnp.bfloat16)
    correlate(win_ref, taps_ref, near_ref, 0, 0, None)

    listed = jnp.concatenate([footprint_ref[...], jnp.full((FOOT, LANE - N_PULSE), -1)], axis=1)
    listed = listed.T
    listed_ref[...] = listed
    places = (slot_ref[...] + 1).astype(jnp.float32)
    lane = lax.broadcasted_iota(jnp.int32, (N_PULSE, LANE), 1)
    slots = jnp.zeros((N_PULSE, LANE), jnp.int32)
    local = jnp.zeros((N_PULSE, 1), jnp.int32)
    for k in range(FOOT):
        same = listed[:N_PULSE, k : k + 1] == lane
        slot = jnp.sum(jnp.where(same, places, 0.0), axis=1, keepdims=True).astype(jnp.int32)
        slots = jnp.where(lane == k, slot, slots)
        owned = (slot > 0) & (((slot - 1) >> 2) == me)
        local = jnp.where(owned, ((slot - 1) & 3) + 1, local)
    slots_ref[...] = slots
    local_ref[...] = jnp.broadcast_to(local, (N_PULSE, LANE))

    mine = own_lanes()
    tiles = jnp.maximum(listed_ref[pl.ds(me, 1), :], 0).astype(jnp.float32)
    kappa = jnp.sum(jnp.where(mine, angle_ref[1:2, :], 0.0), axis=1, keepdims=True)
    phase = jnp.sum(jnp.where(mine, angle_ref[2:3, :], 0.0), axis=1, keepdims=True)
    tiles = jnp.concatenate([tiles, jnp.zeros((1, LANE - FOOT), jnp.float32)], axis=1)
    turn = kappa * tiles + phase
    step = lax.broadcasted_iota(jnp.int32, (P_DEV, PULSES), 0).astype(jnp.float32)
    angles = jnp.concatenate([step * angle_ref[0:1, :], turn], axis=1)
    cosine, sine = jnp.cos(angles), jnp.sin(angles)
    fill_steer(cosine[:, :PULSES], sine[:, :PULSES], steer_ref)
    cosine, sine = cosine[:, PULSES:], sine[:, PULSES:]
    pulse = lax.broadcasted_iota(jnp.int32, (P_DEV, ROWS), 0)
    pick = lax.broadcasted_iota(jnp.int32, (P_DEV, ROWS), 1)
    low_hot, high_hot = [], []
    for k in range(FOOT):
        rows = slice(P_DEV * k, P_DEV * k + P_DEV)
        offset = offset_ref[k : k + 1, :].astype(jnp.float32)
        offset = jnp.sum(jnp.where(mine, offset, 0.0), axis=1, keepdims=True).astype(jnp.int32)
        block = offset >> 8
        low_hot.append(jnp.where(pick == block * P_DEV + pulse, 1.0, 0.0))
        block = jnp.minimum(block + 1, BLOCKS - 1)
        high_hot.append(jnp.where(pick == block * P_DEV + pulse, 1.0, 0.0))
        shift_ref[rows, :] = jnp.broadcast_to(offset & (TILE - 1), (P_DEV, LANE))
        turn_ref[0, rows, :] = jnp.broadcast_to(cosine[:, k : k + 1], (P_DEV, LANE))
        turn_ref[1, rows, :] = jnp.broadcast_to(sine[:, k : k + 1], (P_DEV, LANE))
    hot_ref[...] = jnp.concatenate(low_hot + high_hot, axis=0).astype(jnp.bfloat16)


def correlate(win_ref, taps_ref, out_ref, first_row, first_span, add_ref):
    count = out_ref.shape[1]
    left = []
    for comp in range(2):
        cols = slice(TILE * comp, TILE * comp + 2 * TILE)
        spans = [
            win_ref[first_row + P_DEV * a : first_row + P_DEV * a + count, cols]
            for a in range(first_span, SPANS)
        ]
        left.append(jnp.concatenate(spans, axis=1))
    total = lax.dot_general(
        jnp.concatenate(left, axis=0),
        taps_ref[:, 2 * TILE * first_span :],
        NT,
        preferred_element_type=jnp.float32,
    )
    for comp in range(2):
        part = total[count * comp : count * comp + count]
        out_ref[comp] = part if add_ref is None else part + add_ref[comp, first_row:, :]


def lane_shift(low, high, shift):
    first, second = low[:, :LANE], low[:, LANE:]
    third, fourth = high[:, :LANE], high[:, LANE:]
    far = shift >= LANE
    parts = [
        jnp.where(far, second, first),
        jnp.where(far, third, second),
        jnp.where(far, fourth, third),
    ]
    step = shift & (LANE - 1)
    lane = lax.broadcasted_iota(jnp.int32, first.shape, 1)
    index = (lane + step) & (LANE - 1)
    turned = [jnp.take_along_axis(part, index, axis=1) for part in parts]
    stay = lane < LANE - step
    return jnp.concatenate(
        [jnp.where(stay, turned[0], turned[1]), jnp.where(stay, turned[1], turned[2])], axis=1
    )


def rows_kernel(
    tail_ref,
    taps_ref,
    near_ref,
    hot_ref,
    shift_ref,
    turn_ref,
    slots_ref,
    out_ref,
    win_ref,
    far_ref,
):
    me = lax.axis_index("pulse")
    half = (BLOCKS - SPANS + 1) * P_DEV
    win_ref[:ROWS, :] = jnp.zeros((ROWS, 3 * TILE), jnp.bfloat16)
    for n in range(SPANS - 1):
        rows = slice(ROWS + P_DEV * n, ROWS + P_DEV * n + P_DEV)
        real = tail_ref[0, :, TILE * n : TILE * n + TILE]
        win_ref[rows, :TILE] = real
        win_ref[rows, TILE : 2 * TILE] = tail_ref[1, :, TILE * n : TILE * n + TILE]
        win_ref[rows, 2 * TILE :] = -real
    correlate(win_ref, taps_ref, far_ref, half, 1, near_ref)
    series = jnp.concatenate(
        [
            jnp.concatenate([near_ref[0, :half, :], near_ref[1, :half, :]], axis=1),
            jnp.concatenate([far_ref[0], far_ref[1]], axis=1),
        ],
        axis=0,
    ).astype(jnp.bfloat16)
    picked = lax.dot_general(hot_ref[...], series, NN, preferred_element_type=jnp.float32)
    out_ref[...] = jnp.zeros_like(out_ref)
    for k in reversed(range(FOOT)):
        rows = slice(P_DEV * k, P_DEV * k + P_DEV)
        low = picked[P_DEV * k : P_DEV * k + P_DEV]
        high = picked[P_DEV * (FOOT + k) : P_DEV * (FOOT + k) + P_DEV]
        shift = shift_ref[rows, :]
        real = lane_shift(low[:, :TILE], high[:, :TILE], shift)
        imag = lane_shift(low[:, TILE:], high[:, TILE:], shift)
        c = jnp.concatenate([turn_ref[0, rows, :]] * 2, axis=1)
        s = jnp.concatenate([turn_ref[1, rows, :]] * 2, axis=1)
        slot = slots_ref[me, k]
        owner = (jnp.where(slot > 0, slot, slots_ref[me, 0]) - 1) >> 2
        out_ref[owner, 0] = ((real * c - imag * s) * FACTOR).astype(jnp.bfloat16)
        out_ref[owner, 1] = ((real * s + imag * c) * FACTOR).astype(jnp.bfloat16)


def owner_kernel(
    local_ref,
    arrived_ref,
    steer_ref,
    image_hbm,
    grad_ref,
    rows_ref,
    weight_ref,
    flat_ref,
    image_ref,
    image_sem,
):
    for d in range(N_PULSE):
        slot = local_ref[d, 0]
        for comp in range(2):
            piece = arrived_ref[d, comp]
            row = PULSES * comp + P_DEV * d
            for l in range(TILES_DEV):
                rows_ref[row : row + P_DEV, TILE * l : TILE * l + TILE] = jnp.where(
                    slot == l + 1, piece, jnp.zeros_like(piece)
                )
    copies, sums = [], []

    def write_out(l):
        cols = slice(TILE * l, TILE * l + TILE)
        for c in range(2):
            image_ref[l, c] = flat_ref[TILE * c : TILE * c + TILE, cols].T
            copy = pltpu.make_async_copy(image_ref.at[l, c], image_hbm.at[c, l], image_sem.at[l, c])
            copy.start()
            copies.append(copy)

    for l in range(TILES_DEV):
        cols = slice(TILE * l, TILE * l + TILE)
        total = lax.dot_general(
            steer_ref[...], rows_ref[:, cols], NN, preferred_element_type=jnp.float32
        )
        flat_ref[:, cols] = total
        if l > 0:
            write_out(l - 1)
        real, imag = total[:TILE], total[TILE:]
        power = real * real + imag * imag
        weight_ref[:TILE, cols] = (-power * imag).astype(jnp.bfloat16)
        weight_ref[TILE:, cols] = (power * real).astype(jnp.bfloat16)
    for h in range(KDIM // TILE):
        cols = slice(TILE * h, TILE * h + TILE)
        back = lax.dot_general(
            weight_ref[...], rows_ref[cols, :], NT, preferred_element_type=jnp.float32
        )
        if h == 0:
            write_out(TILES_DEV - 1)
        sums.append(
            jnp.sum(back * steer_ref[:, cols].astype(jnp.float32), axis=0, keepdims=True)
        )
    halves = [-4.0 * (sums[h] + sums[h + 2]) for h in range(2)]
    for c in range(PULSES // LANE):
        grad_ref[c : c + 1, :] = halves[c // 2][:, LANE * (c % 2) : LANE * (c % 2) + LANE]
    for copy in copies:
        copy.wait()


def spread_kernel(own_ref, other_ref, out_ref):
    total = (own_ref[...] + other_ref[...]).astype(jnp.bfloat16)
    for m in range(N_PULSE * N_BAND // 2):
        out_ref[m] = total


def final_kernel(parts_ref, out_ref):
    me = lax.axis_index("pulse")
    gradient = jnp.sum(parts_ref[...].astype(jnp.float32), axis=0)
    square = jnp.sum(jnp.sum(gradient * gradient, axis=0, keepdims=True), axis=1, keepdims=True)
    scaled = gradient / jnp.sqrt(square / PULSES + 1e-05)
    row = lax.broadcasted_iota(jnp.int32, scaled.shape, 0)
    own = jnp.sum(jnp.where(row == me >> 3, scaled, 0.0), axis=0, keepdims=True)
    turned = pltpu.roll(jnp.broadcast_to(own, (8, LANE)), (LANE - P_DEV * (me & 7)) & (LANE - 1), 1)
    out_ref[...] = turned[:1, :P_DEV]


def kernel(body, name, out_shape, scratch=(), cost=None, **extra):
    return pl.pallas_call(
        body,
        out_shape=out_shape,
        scratch_shapes=list(scratch),
        compiler_params=pltpu.CompilerParams(vmem_limit_bytes=VMEM_BYTES),
        cost_estimate=pl.CostEstimate(flops=0, bytes_accessed=cost, transcendentals=0) if cost else None,
        name=name,
        **extra,
    )


def on_device(echoes, replica, pulse_angles, footprint, tile_slot, offsets):
    bf16, f32, i32 = jnp.bfloat16, jnp.float32, jnp.int32
    shape = jax.ShapeDtypeStruct
    window = pltpu.VMEM((ROWS + P_DEV * (SPANS - 1), 3 * TILE), bf16)
    tail = lax.ppermute(echoes[:, :, :TAPS], "band", [(i, i - 1) for i in range(1, N_BAND)])
    taps = kernel(
        taps_kernel, "taps", shape((TILE, 2 * TILE * SPANS), bf16), cost=8 << 20
    )(replica)
    steer, slots, local, hot, shift, turn, near = kernel(
        prep_kernel,
        "prep",
        [
            shape((2 * TILE, KDIM), bf16),
            shape((N_PULSE, LANE), i32),
            shape((N_PULSE, LANE), i32),
            shape((ROWS, ROWS), bf16),
            shape((ROWS // 2, LANE), i32),
            shape((2, ROWS // 2, LANE), f32),
            shape((2, ROWS, TILE), f32),
        ],
        scratch=[window, pltpu.VMEM((LANE, FOOT), i32)],
        cost=12 << 20,
    )(taps, echoes, pulse_angles, footprint.T, tile_slot.reshape(1, NTILE), offsets.T)
    rows = kernel(
        rows_kernel,
        "rows",
        shape((N_PULSE, 2, P_DEV, TILE), bf16),
        scratch=[window, pltpu.VMEM((2, (SPANS - 1) * P_DEV, TILE), f32)],
    )(tail, taps, near, hot, shift, turn, slots)
    arrived = lax.all_to_all(rows, "pulse", split_axis=0, concat_axis=0, tiled=True)
    image, grad = kernel(
        owner_kernel,
        "owner",
        [
            shape((2, TILES_DEV, TILE, TILE), f32),
            shape((PULSES // LANE, LANE), f32),
        ],
        out_specs=[pl.BlockSpec(memory_space=pl.ANY), pl.BlockSpec(memory_space=pltpu.VMEM)],
        scratch=[
            pltpu.VMEM((KDIM, TILES_DEV * TILE), bf16),
            pltpu.VMEM((2 * TILE, TILES_DEV * TILE), bf16),
            pltpu.VMEM((2 * TILE, TILES_DEV * TILE), f32),
            pltpu.VMEM((TILES_DEV, 2, TILE, TILE), f32),
            pltpu.SemaphoreType.DMA((TILES_DEV, 2)),
        ],
    )(local, arrived, steer)
    other = lax.ppermute(grad, "band", [(i, i ^ 1) for i in range(N_BAND)])
    chips = N_PULSE * N_BAND // 2
    spread = kernel(spread_kernel, "spread", shape((chips, PULSES // LANE, LANE), bf16))(
        grad, other
    )
    parts = lax.all_to_all(
        spread,
        ("pulse", "band"),
        split_axis=0,
        concat_axis=0,
        axis_index_groups=[list(range(core, 2 * chips, 2)) for core in range(2)],
        tiled=True,
    )
    own = kernel(final_kernel, "final", shape((1, P_DEV), f32))(parts)
    return (image, own.reshape(P_DEV))


def solution(mesh):
    placed = (P(None, "pulse", "band"), P(), P(), P(), P(), P())
    return jax.shard_map(
        on_device,
        mesh=mesh,
        in_specs=placed,
        out_specs=(P(None, "pulse", "band", None), P("pulse")),
        check_vma=False,
    )
```

```python
import math

import jax
import jax.numpy as jnp
from jax import lax
from jax.experimental import pallas as pl
from jax.experimental.pallas import tpu as pltpu
from jax.sharding import PartitionSpec as P

TILE = 256
TAPS = 2048
RB = 4096
P_DEV = 16
FOOT = 8
TILES_DEV = 4
NTILE = 128
PULSES = 512
N_PULSE = 32
N_BAND = 8
LANE = 128

SPANS = TAPS // TILE + 1
BLOCKS = RB // TILE
ROWS = BLOCKS * P_DEV
KDIM = 2 * PULSES
FACTOR = 0.5 / math.sqrt(P_DEV)

NT = (((1,), (1,)), ((), ()))
NN = (((1,), (0,)), ((), ()))

VMEM_BYTES = 24 * 1024 * 1024


def taps_kernel(replica_ref, taps_ref):
    width = TAPS + LANE
    chunks = width // LANE
    zero = jnp.zeros((16, LANE), jnp.bfloat16)
    for comp in range(2):
        line = replica_ref[comp : comp + 1, :].astype(jnp.float32)
        line = jnp.concatenate([line, jnp.zeros((1, LANE), jnp.float32)], axis=1)
        wide = jnp.broadcast_to(line, (8, width))
        base = pltpu.roll(wide, 0, 1, stride=1, stride_axis=0)
        for j in range(8):
            first = base if j == 0 else pltpu.roll(base, 16 * j, 1)
            pair = jnp.concatenate([first, pltpu.roll(base, 16 * j + 8, 1)], axis=0)
            pair = pair.astype(jnp.bfloat16)
            for half in range(2):
                row = LANE * half + 16 * j
                for c in range(2 * SPANS):
                    src = c - half
                    piece = pair[:, LANE * src : LANE * src + LANE] if 0 <= src < chunks else zero
                    col = 512 * (c // 2) + TILE * comp + LANE * (c % 2)
                    taps_ref[row : row + 16, col : col + LANE] = piece


def fill_steer(angle_ref, steer_ref):
    step = lax.broadcasted_iota(jnp.int32, (16, PULSES), 0).astype(jnp.float32)
    omega = angle_ref[0:1, :]
    fine, coarse = step * omega, (16.0 * step) * omega
    fine_cos, fine_sin = jnp.cos(fine), jnp.sin(fine)
    coarse_cos, coarse_sin = jnp.cos(coarse), jnp.sin(coarse)
    for a in range(TILE // 16):
        ca, sa = coarse_cos[a : a + 1], coarse_sin[a : a + 1]
        cosine = (fine_cos * ca - fine_sin * sa).astype(jnp.bfloat16)
        sine = (fine_sin * ca + fine_cos * sa).astype(jnp.bfloat16)
        upper, lower = slice(16 * a, 16 * a + 16), slice(TILE + 16 * a, TILE + 16 * a + 16)
        steer_ref[upper, :PULSES] = cosine
        steer_ref[upper, PULSES:] = -sine
        steer_ref[lower, :PULSES] = sine
        steer_ref[lower, PULSES:] = cosine


def own_lanes():
    lane = lax.broadcasted_iota(jnp.int32, (P_DEV, PULSES), 1)
    sub = lax.broadcasted_iota(jnp.int32, (P_DEV, PULSES), 0)
    return lane == lax.axis_index("pulse") * P_DEV + sub


def prep_kernel(
    taps_ref,
    echo_ref,
    angle_ref,
    footprint_ref,
    slot_ref,
    offset_ref,
    steer_ref,
    slots_ref,
    local_ref,
    hot_ref,
    shift_ref,
    turn_ref,
    near_ref,
    win_ref,
    listed_ref,
):
    me = lax.axis_index("pulse")
    fill_steer(angle_ref, steer_ref)

    for n in range(BLOCKS):
        rows = slice(P_DEV * n, P_DEV * n + P_DEV)
        real = echo_ref[0, :, TILE * n : TILE * n + TILE]
        win_ref[rows, :TILE] = real
        win_ref[rows, TILE : 2 * TILE] = echo_ref[1, :, TILE * n : TILE * n + TILE]
        win_ref[rows, 2 * TILE :] = -real
    win_ref[ROWS:, :] = jnp.zeros((P_DEV * (SPANS - 1), 3 * TILE), jnp.bfloat16)
    correlate(win_ref, taps_ref, near_ref, 0, 0, None)

    listed = jnp.concatenate([footprint_ref[...], jnp.full((FOOT, LANE - N_PULSE), -1)], axis=1)
    listed = listed.T
    listed_ref[...] = listed
    places = (slot_ref[...] + 1).astype(jnp.float32)
    lane = lax.broadcasted_iota(jnp.int32, (N_PULSE, LANE), 1)
    slots = jnp.zeros((N_PULSE, LANE), jnp.int32)
    local = jnp.zeros((N_PULSE, 1), jnp.int32)
    for k in range(FOOT):
        same = listed[:N_PULSE, k : k + 1] == lane
        slot = jnp.sum(jnp.where(same, places, 0.0), axis=1, keepdims=True).astype(jnp.int32)
        slots = jnp.where(lane == k, slot, slots)
        owned = (slot > 0) & (((slot - 1) >> 2) == me)
        local = jnp.where(owned, ((slot - 1) & 3) + 1, local)
    slots_ref[...] = slots
    local_ref[...] = jnp.broadcast_to(local, (N_PULSE, LANE))

    mine = own_lanes()
    tiles = jnp.maximum(listed_ref[pl.ds(me, 1), :], 0).astype(jnp.float32)
    kappa = jnp.sum(jnp.where(mine, angle_ref[1:2, :], 0.0), axis=1, keepdims=True)
    phase = jnp.sum(jnp.where(mine, angle_ref[2:3, :], 0.0), axis=1, keepdims=True)
    turn = kappa * tiles + phase
    cosine, sine = jnp.cos(turn), jnp.sin(turn)
    pulse = lax.broadcasted_iota(jnp.int32, (P_DEV, ROWS), 0)
    pick = lax.broadcasted_iota(jnp.int32, (P_DEV, ROWS), 1)
    low_hot, high_hot = [], []
    for k in range(FOOT):
        rows = slice(P_DEV * k, P_DEV * k + P_DEV)
        offset = offset_ref[k : k + 1, :].astype(jnp.float32)
        offset = jnp.sum(jnp.where(mine, offset, 0.0), axis=1, keepdims=True).astype(jnp.int32)
        block = offset >> 8
        low_hot.append(jnp.where(pick == block * P_DEV + pulse, 1.0, 0.0))
        block = jnp.minimum(block + 1, BLOCKS - 1)
        high_hot.append(jnp.where(pick == block * P_DEV + pulse, 1.0, 0.0))
        shift_ref[rows, :] = jnp.broadcast_to(offset & (TILE - 1), (P_DEV, LANE))
        turn_ref[0, rows, :] = jnp.broadcast_to(cosine[:, k : k + 1], (P_DEV, LANE))
        turn_ref[1, rows, :] = jnp.broadcast_to(sine[:, k : k + 1], (P_DEV, LANE))
    hot_ref[...] = jnp.concatenate(low_hot + high_hot, axis=0).astype(jnp.bfloat16)


def correlate(win_ref, taps_ref, out_ref, first_row, first_span, add_ref):
    count = out_ref.shape[1]
    left = []
    for comp in range(2):
        cols = slice(TILE * comp, TILE * comp + 2 * TILE)
        spans = [
            win_ref[first_row + P_DEV * a : first_row + P_DEV * a + count, cols]
            for a in range(first_span, SPANS)
        ]
        left.append(jnp.concatenate(spans, axis=1))
    total = lax.dot_general(
        jnp.concatenate(left, axis=0),
        taps_ref[:, 2 * TILE * first_span :],
        NT,
        preferred_element_type=jnp.float32,
    )
    for comp in range(2):
        part = total[count * comp : count * comp + count]
        out_ref[comp] = part if add_ref is None else part + add_ref[comp, first_row:, :]


def lane_shift(low, high, shift):
    first, second = low[:, :LANE], low[:, LANE:]
    third, fourth = high[:, :LANE], high[:, LANE:]
    far = shift >= LANE
    parts = [
        jnp.where(far, second, first),
        jnp.where(far, third, second),
        jnp.where(far, fourth, third),
    ]
    step = shift & (LANE - 1)
    lane = lax.broadcasted_iota(jnp.int32, first.shape, 1)
    index = (lane + step) & (LANE - 1)
    turned = [jnp.take_along_axis(part, index, axis=1) for part in parts]
    stay = lane < LANE - step
    return jnp.concatenate(
        [jnp.where(stay, turned[0], turned[1]), jnp.where(stay, turned[1], turned[2])], axis=1
    )


def rows_kernel(
    tail_ref,
    taps_ref,
    near_ref,
    hot_ref,
    shift_ref,
    turn_ref,
    slots_ref,
    out_ref,
    win_ref,
    far_ref,
):
    me = lax.axis_index("pulse")
    half = (BLOCKS - SPANS + 1) * P_DEV
    win_ref[:ROWS, :] = jnp.zeros((ROWS, 3 * TILE), jnp.bfloat16)
    for n in range(SPANS - 1):
        rows = slice(ROWS + P_DEV * n, ROWS + P_DEV * n + P_DEV)
        real = tail_ref[0, :, TILE * n : TILE * n + TILE]
        win_ref[rows, :TILE] = real
        win_ref[rows, TILE : 2 * TILE] = tail_ref[1, :, TILE * n : TILE * n + TILE]
        win_ref[rows, 2 * TILE :] = -real
    correlate(win_ref, taps_ref, far_ref, half, 1, near_ref)
    series = jnp.concatenate(
        [
            jnp.concatenate([near_ref[0, :half, :], near_ref[1, :half, :]], axis=1),
            jnp.concatenate([far_ref[0], far_ref[1]], axis=1),
        ],
        axis=0,
    ).astype(jnp.bfloat16)
    picked = lax.dot_general(hot_ref[...], series, NN, preferred_element_type=jnp.float32)
    out_ref[...] = jnp.zeros_like(out_ref)
    for k in reversed(range(FOOT)):
        rows = slice(P_DEV * k, P_DEV * k + P_DEV)
        low = picked[P_DEV * k : P_DEV * k + P_DEV]
        high = picked[P_DEV * (FOOT + k) : P_DEV * (FOOT + k) + P_DEV]
        shift = shift_ref[rows, :]
        real = lane_shift(low[:, :TILE], high[:, :TILE], shift)
        imag = lane_shift(low[:, TILE:], high[:, TILE:], shift)
        c = jnp.concatenate([turn_ref[0, rows, :]] * 2, axis=1)
        s = jnp.concatenate([turn_ref[1, rows, :]] * 2, axis=1)
        slot = slots_ref[me, k]
        owner = (jnp.where(slot > 0, slot, slots_ref[me, 0]) - 1) >> 2
        out_ref[owner, 0] = ((real * c - imag * s) * FACTOR).astype(jnp.bfloat16)
        out_ref[owner, 1] = ((real * s + imag * c) * FACTOR).astype(jnp.bfloat16)


def owner_kernel(
    local_ref,
    arrived_ref,
    steer_ref,
    flat_ref,
    grad_ref,
    rows_ref,
    weight_ref,
):
    for d in range(N_PULSE):
        slot = local_ref[d, 0]
        for comp in range(2):
            piece = arrived_ref[d, comp]
            row = PULSES * comp + P_DEV * d
            for l in range(TILES_DEV):
                rows_ref[row : row + P_DEV, TILE * l : TILE * l + TILE] = jnp.where(
                    slot == l + 1, piece, jnp.zeros_like(piece)
                )
    sums = []
    for l in range(TILES_DEV):
        cols = slice(TILE * l, TILE * l + TILE)
        total = lax.dot_general(
            steer_ref[...], rows_ref[:, cols], NN, preferred_element_type=jnp.float32
        )
        flat_ref[:, cols] = total
        real, imag = total[:TILE], total[TILE:]
        power = real * real + imag * imag
        weight_ref[:TILE, cols] = (-power * imag).astype(jnp.bfloat16)
        weight_ref[TILE:, cols] = (power * real).astype(jnp.bfloat16)
    for h in range(KDIM // TILE):
        cols = slice(TILE * h, TILE * h + TILE)
        back = lax.dot_general(
            weight_ref[...], rows_ref[cols, :], NT, preferred_element_type=jnp.float32
        )
        sums.append(
            jnp.sum(back * steer_ref[:, cols].astype(jnp.float32), axis=0, keepdims=True)
        )
    halves = [-4.0 * (sums[h] + sums[h + 2]) for h in range(2)]
    for c in range(PULSES // LANE):
        grad_ref[c : c + 1, :] = halves[c // 2][:, LANE * (c % 2) : LANE * (c % 2) + LANE]


def image_kernel(flat_ref, spread_ref, out_ref):
    for comp in range(2):
        out_ref[comp, 0] = flat_ref[TILE * comp : TILE * comp + TILE, :].T


def spread_kernel(own_ref, other_ref, out_ref):
    total = (own_ref[...] + other_ref[...]).astype(jnp.bfloat16)
    for m in range(N_PULSE * N_BAND // 2):
        out_ref[m] = total


def final_kernel(parts_ref, out_ref):
    me = lax.axis_index("pulse")
    gradient = jnp.sum(parts_ref[...].astype(jnp.float32), axis=0)
    square = jnp.sum(jnp.sum(gradient * gradient, axis=0, keepdims=True), axis=1, keepdims=True)
    scaled = gradient / jnp.sqrt(square / PULSES + 1e-05)
    row = lax.broadcasted_iota(jnp.int32, scaled.shape, 0)
    own = jnp.sum(jnp.where(row == me >> 3, scaled, 0.0), axis=0, keepdims=True)
    turned = pltpu.roll(jnp.broadcast_to(own, (8, LANE)), (LANE - P_DEV * (me & 7)) & (LANE - 1), 1)
    out_ref[...] = turned[:1, :P_DEV]


def kernel(body, name, out_shape, scratch=(), cost=None, **extra):
    return pl.pallas_call(
        body,
        out_shape=out_shape,
        scratch_shapes=list(scratch),
        compiler_params=pltpu.CompilerParams(vmem_limit_bytes=VMEM_BYTES),
        cost_estimate=pl.CostEstimate(flops=0, bytes_accessed=cost, transcendentals=0) if cost else None,
        name=name,
        **extra,
    )


def on_device(echoes, replica, pulse_angles, footprint, tile_slot, offsets):
    bf16, f32, i32 = jnp.bfloat16, jnp.float32, jnp.int32
    shape = jax.ShapeDtypeStruct
    window = pltpu.VMEM((ROWS + P_DEV * (SPANS - 1), 3 * TILE), bf16)
    tail = lax.ppermute(echoes[:, :, :TAPS], "band", [(i, i - 1) for i in range(1, N_BAND)])
    taps = kernel(
        taps_kernel, "taps", shape((TILE, 2 * TILE * SPANS), bf16), cost=8 << 20
    )(replica)
    steer, slots, local, hot, shift, turn, near = kernel(
        prep_kernel,
        "prep",
        [
            shape((2 * TILE, KDIM), bf16),
            shape((N_PULSE, LANE), i32),
            shape((N_PULSE, LANE), i32),
            shape((ROWS, ROWS), bf16),
            shape((ROWS // 2, LANE), i32),
            shape((2, ROWS // 2, LANE), f32),
            shape((2, ROWS, TILE), f32),
        ],
        scratch=[window, pltpu.VMEM((LANE, FOOT), i32)],
        cost=12 << 20,
    )(taps, echoes, pulse_angles, footprint.T, tile_slot.reshape(1, NTILE), offsets.T)
    rows = kernel(
        rows_kernel,
        "rows",
        shape((N_PULSE, 2, P_DEV, TILE), bf16),
        scratch=[window, pltpu.VMEM((2, (SPANS - 1) * P_DEV, TILE), f32)],
    )(tail, taps, near, hot, shift, turn, slots)
    arrived = lax.all_to_all(rows, "pulse", split_axis=0, concat_axis=0, tiled=True)
    flat, grad = kernel(
        owner_kernel,
        "owner",
        [
            shape((2 * TILE, TILES_DEV * TILE), f32),
            shape((PULSES // LANE, LANE), f32),
        ],
        scratch=[
            pltpu.VMEM((KDIM, TILES_DEV * TILE), bf16),
            pltpu.VMEM((2 * TILE, TILES_DEV * TILE), bf16),
        ],
    )(local, arrived, steer)
    other = lax.ppermute(grad, "band", [(i, i ^ 1) for i in range(N_BAND)])
    chips = N_PULSE * N_BAND // 2
    spread = kernel(spread_kernel, "spread", shape((chips, PULSES // LANE, LANE), bf16))(
        grad, other
    )
    image = kernel(
        image_kernel,
        "image",
        shape((2, TILES_DEV, TILE, TILE), f32),
        grid=(TILES_DEV,),
        in_specs=[
            pl.BlockSpec((2 * TILE, TILE), lambda l: (0, l)),
            pl.BlockSpec(memory_space=pl.ANY),
        ],
        out_specs=pl.BlockSpec((2, 1, TILE, TILE), lambda l: (0, l, 0, 0)),
    )(flat, spread)
    parts = lax.all_to_all(
        spread,
        ("pulse", "band"),
        split_axis=0,
        concat_axis=0,
        axis_index_groups=[list(range(core, 2 * chips, 2)) for core in range(2)],
        tiled=True,
    )
    own = kernel(final_kernel, "final", shape((1, P_DEV), f32))(parts)
    return (image, own.reshape(P_DEV))


def solution(mesh):
    placed = (P(None, "pulse", "band"), P(), P(), P(), P(), P())
    return jax.shard_map(
        on_device,
        mesh=mesh,
        in_specs=placed,
        out_specs=(P(None, "pulse", "band", None), P("pulse")),
        check_vma=False,
    )
```
